32 devices in a mesh: grp: 2 (over y), tok: 16 (over z, x, core).
Axes of the slice: x: 2, y: 2, z: 4, core: 2. Of those that a mesh axis runs over, the one named last changes fastest.
Arguments:
- hidden: bfloat16 [4, 1024, 1536], P('grp', 'tok'), parts along dimension 0
- base_ids: int32 [4, 1024], P('grp', 'tok'), parts along dimension 0, may hold values from 0 to 4, as said below
- attn_gain: bfloat16 [1536], replicated, may hold values from 0.099609375 to 1.8984375
- q_weight: bfloat16 [1536, 768], replicated
- kv_weight: bfloat16 [1536, 384], replicated
- out_weight: bfloat16 [768, 1536], replicated, may hold values from -0.21875 to 0.21875
- head_gain: bfloat16 [1536], replicated, may hold values from 0.099609375 to 1.8984375
- head_weight: bfloat16 [1536, 1536], replicated, may hold values from -0.15625 to 0.15625
- head_bias: float32 [1536], replicated, may hold values from -1 to 1
- track_perm: int32 [1536], replicated, may hold values from 0 to 1535, each once
Outputs:
- combined: float32 [2048, 1536], P(('grp', 'tok')), parts along dimension 0
The draws below stay inside these ranges and needn't reach their ends.
There are 2 independent parts, one for each index of `grp`. The reference program is written for one: setup_inputs(seed, part) draws one part's arguments, and reference() takes and returns one part's arrays. A program takes and returns all parts, laid end to end along the dimension named above; an argument that names none is the same for every part. Nothing has to cross between parts.
Inputs may be any that keep to these rules, and one draw needn't show every extreme that they name: `base_ids`: every eighth token of each strand, from token 0, has a base 0 to 3.
All inputs are finite; a program needn't handle non-finite values.
Results may differ from the reference program's by a relative error of at most 0.0058.
Values may be sent and summed in bfloat16 or wider, within the bound.
A program may use at most 128 MiB of HBM per device.

```python
import math
import jax
import jax.numpy as jnp
from jax import lax

D = 1536
HEADS = 4
DH = 192
TRACKS = 1536
TOK_DEV = 64
LENGTH = 1024
N_TOK = 16


def shared_key_cols(key):
    return jax.random.normal(jax.random.fold_in(key, 11), (D, DH), jnp.float32) * D ** (-0.5)


def draw_kv_weight(key, part):
    key_cols = shared_key_cols(key)
    value_cols = jax.random.normal(jax.random.fold_in(key, 12), (D, DH), jnp.float32) * D ** (-0.5)
    return jnp.concatenate([key_cols, value_cols], axis=1).astype(jnp.bfloat16)


def draw_q_weight(key, part):
    jitter = jax.random.normal(jax.random.fold_in(key, 13), (D, HEADS, DH), jnp.float32) * D ** (-0.5)
    result = jitter
    return result.reshape(D, HEADS * DH).astype(jnp.bfloat16)


def draw_hidden(key, part):
    result = jax.random.normal(jax.random.fold_in(key, 24), (2, LENGTH, D), jnp.float32)
    return result.astype(jnp.bfloat16)


def draw_base_ids(key, part):
    raw_ids = jax.random.randint(jax.random.fold_in(key, 31), (2, LENGTH), 0, 5)
    safe_ids = jax.random.randint(jax.random.fold_in(key, 32), (2, LENGTH), 0, 4)
    position = jnp.arange(LENGTH)[None, :]
    return jnp.where(position % 8 == 0, safe_ids, raw_ids).astype(jnp.int32)


def noise(own_key, dims, deviation, bound, kind=jnp.bfloat16):
    values = deviation * jax.random.normal(own_key, dims, jnp.float32)
    return jnp.clip(values, min=-bound, max=bound).astype(kind)


def setup_inputs(seed: int = 0, part: int = 0) -> dict:
    key_of = jax.random.split(jax.random.key(seed), 11)
    part_keys = jax.random.split(jax.random.fold_in(key_of[10], part), 11)
    return {
        "hidden": draw_hidden(jax.random.fold_in(jax.random.fold_in(key_of[10], part), 71), part),
        "base_ids": draw_base_ids(jax.random.fold_in(jax.random.fold_in(key_of[10], part), 71), part),
        "attn_gain": jnp.clip(1.0 + 0.18 * jax.random.normal(key_of[2], (D,), jnp.float32), 0.099609375, 1.8984375).astype(jnp.bfloat16),
        "q_weight": draw_q_weight(jax.random.fold_in(key_of[10], 71), part),
        "kv_weight": draw_kv_weight(jax.random.fold_in(key_of[10], 71), part),
        "out_weight": noise(key_of[5], (HEADS * DH, D), (HEADS * DH) ** -0.5, 0.21875),
        "head_gain": jnp.clip(1.0 + 0.18 * jax.random.normal(key_of[6], (D,), jnp.float32), 0.099609375, 1.8984375).astype(jnp.bfloat16),
        "head_weight": noise(key_of[7], (D, TRACKS), D ** -0.5, 0.15625),
        "head_bias": jnp.clip(jax.random.uniform(key_of[8], (TRACKS,), jnp.float32, -1.0, 1.0), -1.0, 1.0),
        "track_perm": jax.random.permutation(key_of[9], TRACKS).astype(jnp.int32),
    }


def normalize(rows, gain):
    widened = rows.astype(jnp.float32)
    return widened * lax.rsqrt(lax.optimization_barrier(jnp.mean(widened * widened, -1, keepdims=True)) + 1e-06) * gain.astype(jnp.float32)

def reference(hidden, base_ids, attn_gain, q_weight, kv_weight, out_weight, head_gain, head_weight, head_bias, track_perm):
    score_scale = 1.0 / math.sqrt(DH)
    predictions = []
    for strand in range(2):
        normed = normalize(hidden[strand], attn_gain).astype(jnp.bfloat16)
        queries = jnp.dot(normed, q_weight, preferred_element_type=jnp.float32).astype(jnp.bfloat16)
        queries = queries.reshape(N_TOK, TOK_DEV * HEADS, DH)
        key_value = jnp.dot(normed, kv_weight, preferred_element_type=jnp.float32).astype(jnp.bfloat16)
        key_rows = key_value[:, :DH]
        value_rows = key_value[:, DH:]
        usable = (base_ids[strand] != 4)[None, :]

        def query_block(query_rows):
            scores = jnp.dot(query_rows, key_rows.T, preferred_element_type=jnp.float32) * score_scale
            scores = jnp.where(usable, scores, jnp.float32(-1e+30))
            maxima = lax.optimization_barrier(jnp.max(scores, -1, keepdims=True))
            weight_exp = jnp.where(usable, jnp.exp(scores - maxima), jnp.float32(0.0))
            totals = lax.optimization_barrier(jnp.sum(weight_exp, -1, keepdims=True))
            rounded = lax.optimization_barrier(weight_exp.astype(jnp.bfloat16))
            summed = jnp.dot(rounded, value_rows, preferred_element_type=jnp.float32)
            return (summed / totals).astype(jnp.bfloat16)
        attended = lax.map(query_block, queries).reshape(LENGTH, HEADS * DH)
        residual_sum = hidden[strand].astype(jnp.float32) + jnp.dot(attended, out_weight, preferred_element_type=jnp.float32)
        normed_out = normalize(residual_sum, head_gain).astype(jnp.bfloat16)
        track_logits = jnp.dot(normed_out, head_weight, preferred_element_type=jnp.float32) + head_bias
        predictions.append(jax.nn.softplus(track_logits).astype(jnp.bfloat16))
    reverse_side = predictions[1][::-1][:, track_perm]
    return 0.5 * (predictions[0].astype(jnp.float32) + reverse_side.astype(jnp.float32))
```

```python
import functools
import math

import jax
import jax.numpy as jnp
from jax import lax
from jax.experimental import pallas as pl
from jax.experimental.pallas import tpu as pltpu
from jax.sharding import PartitionSpec as P

MESH = pl.DeviceIdType.MESH
LANES = 128
FLAG_ROWS = 16


def normalize(rows, gain):
    widened = rows.astype(jnp.float32)
    mean = jnp.mean(widened * widened, -1, keepdims=True)
    return (widened * lax.rsqrt(mean + 1e-06) * gain.astype(jnp.float32)).astype(jnp.bfloat16)


def dot(a, b):
    return jnp.dot(a, b, preferred_element_type=jnp.float32)


def dot_t(a, b):
    return lax.dot_general(a, b, (((1,), (1,)), ((), ())), preferred_element_type=jnp.float32)


def softplus(v):
    return jnp.maximum(v, 0.0) + jnp.log1p(jnp.exp(-jnp.abs(v)))


def kernel(
    n,
    hidden_ref,
    ids_ref,
    attn_gain_ref,
    q_hbm,
    kv_hbm,
    out_hbm,
    head_gain_ref,
    head_hbm,
    bias_ref,
    perm_ref,
    result_ref,
    hid,
    partner_hid,
    kv_w,
    q_w,
    out_w,
    head_w,
    perm_w,
    buf0,
    buf1,
    scores,
    att,
    fwd_pred,
    load_sem,
    out_sem,
    swap_sem,
    recv,
    send_l,
    send_r,
    send_x,
    send_c,
):
    bufs = (buf0, buf1)
    line = n // 4
    rows, width = hid.shape[1], hid.shape[2]
    tracks = head_w.shape[1]
    head_dim = kv_w.shape[1] // 2
    heads = q_w.shape[1] // head_dim
    padded = att.shape[1] // heads
    pad = padded - head_dim
    kv_tiles = kv_w.shape[1] // LANES
    me = lax.axis_index("tok")
    core = lax.rem(me, 2)
    x = lax.rem(me // 2, 2)
    z = me // 4
    left, right = me - 4, me + 4
    across, sibling, partner = me + 2 - 4 * x, me + 1 - 2 * core, n - 1 - me

    def slot(zc, xc, cc):
        return (zc * 2 + xc) * 2 + cc

    loads = [
        pltpu.make_async_copy(hidden_ref, hid, load_sem.at[0]),
        pltpu.make_async_copy(kv_hbm, kv_w, load_sem.at[1]),
        pltpu.make_async_copy(q_hbm, q_w, load_sem.at[2]),
    ]
    loads += [
        pltpu.make_async_copy(
            out_hbm.at[pl.ds(h * head_dim, head_dim)],
            out_w.at[pl.ds(h * padded + pad, head_dim)],
            out_sem.at[h],
        )
        for h in range(heads)
    ]
    loads += [pltpu.make_async_copy(head_hbm, head_w, load_sem.at[3])]
    for load in loads:
        load.start()

    barrier = pltpu.get_barrier_semaphore()

    def greet(device):
        pl.semaphore_signal(barrier, inc=1, device_id={"tok": device}, device_id_type=MESH)

    has_left, has_right = z > 0, z < line - 1
    for device in (across, sibling, partner):
        greet(device)
    pl.when(has_left)(lambda: greet(left))
    pl.when(has_right)(lambda: greet(right))
    pl.semaphore_wait(
        barrier, 3 + has_left.astype(jnp.int32) + has_right.astype(jnp.int32)
    )

    swap = pltpu.make_async_remote_copy(
        src_ref=hidden_ref.at[1],
        dst_ref=partner_hid,
        send_sem=swap_sem.at[0],
        recv_sem=swap_sem.at[1],
        device_id={"tok": partner},
        device_id_type=MESH,
    )
    swap.start()

    def piece(s, index, device, send_sem):
        return pltpu.make_async_remote_copy(
            src_ref=bufs[s].at[index],
            dst_ref=bufs[s].at[index],
            send_sem=send_sem,
            recv_sem=recv.at[s, index],
            device_id={"tok": device},
            device_id_type=MESH,
        )

    def to_left(s, zc):
        return piece(s, slot(zc, x, core), left, send_l.at[s, zc])

    def to_right(s, zc):
        return piece(s, slot(zc, x, core), right, send_r.at[s, zc])

    def to_across(s, zc):
        return piece(s, slot(zc, x, core), across, send_x.at[s, zc])

    def to_sibling(s, zc, xc):
        return piece(s, slot(zc, xc, core), sibling, send_c.at[s, zc * 2 + xc])

    loads[0].wait()
    gain = attn_gain_ref[...]
    normed = normalize(hid[...].reshape(2 * rows, width), gain)
    loads[1].wait()
    key_value = dot(normed, kv_w[...]).astype(jnp.bfloat16)
    flag = jnp.where(ids_ref[...] != 4, 1.0, 0.0).astype(jnp.float32)
    per_tile = LANES // rows
    lane = lax.broadcasted_iota(jnp.int32, (2, LANES), 1)
    start = lax.rem(me, per_tile) * rows
    spread = jnp.concatenate([flag] * per_tile, axis=1)
    spread = jnp.where((lane >= start) & (lane < start + rows), spread, 0.0)
    spread = jnp.concatenate([spread, jnp.zeros((FLAG_ROWS - 2, LANES), jnp.float32)], axis=0)
    buf0[me, pl.ds(kv_tiles * rows, FLAG_ROWS), :] = spread.astype(jnp.bfloat16)
    for s in range(2):
        for j in range(kv_tiles):
            bufs[s][me, pl.ds(j * rows, rows), :] = key_value[
                s * rows : (s + 1) * rows, j * LANES : (j + 1) * LANES
            ]
        pl.when(has_left)(lambda: to_left(s, z).start())
        pl.when(has_right)(lambda: to_right(s, z).start())
        to_across(s, z).start()
        to_sibling(s, z, x).start()

    def project_queries(normed_rows):
        q = dot(normed_rows, q_w[...])
        pieces = []
        inside = lax.broadcasted_iota(jnp.int32, (rows, padded), 1) < head_dim
        for h in range(heads):
            base = h * head_dim // LANES * LANES
            shift = h * head_dim - base
            window = q[:, base : base + padded]
            if shift:
                window = pltpu.roll(window, padded - shift, axis=1)
            pieces.append(jnp.where(inside, window, 0.0))
        return jnp.concatenate(pieces, axis=0).astype(jnp.bfloat16)

    loads[2].wait()
    q0 = project_queries(normed[:rows])

    def build_perm(i, _):
        step = perm_w.shape[0] // 4
        chunk = 128
        for k in range(step // chunk):
            base = i * step + k * chunk
            ids = lax.broadcasted_iota(jnp.int32, (chunk, tracks), 0) + base
            hit = jnp.where(ids == perm_ref[...], 1.0, 0.0)
            perm_w[pl.ds(pl.multiple_of(base, chunk), chunk), :] = hit.astype(jnp.bfloat16)
        return 0

    def hop(d):
        for s in range(2):

            @pl.when(z - d >= 0)
            def _():
                zc = z - d
                to_right(s, zc).wait_recv()
                pl.when(has_right)(lambda: to_right(s, zc).start())
                to_across(s, zc).start()
                to_sibling(s, zc, x).start()

            @pl.when(z + d < line)
            def _():
                zc = z + d
                to_left(s, zc).wait_recv()
                pl.when(has_left)(lambda: to_left(s, zc).start())
                to_across(s, zc).start()
                to_sibling(s, zc, x).start()

    if line <= 4:
        for d in range(1, line):
            hop(d)
            build_perm(d - 1, 0)
        for i in range(line - 1, 4):
            build_perm(i, 0)
    else:

        @pl.loop(1, line)
        def _(d):
            hop(d)

        lax.fori_loop(0, 4, build_perm, 0)
    out_zero = jnp.zeros((pad, width), jnp.bfloat16)
    for h in range(heads):
        out_w[pl.ds(h * padded, pad), :] = out_zero

    for s in range(2):

        @pl.loop(0, line)
        def _(zc):
            piece(s, slot(zc, 1 - x, core), across, send_x.at[s, zc]).wait_recv()
            to_sibling(s, zc, 1 - x).start()

    def wait_sibling(s):
        @pl.loop(0, line)
        def _(zc):
            for xc in range(2):
                piece(
                    s, slot(zc, xc, 1 - core), sibling, send_c.at[s, zc * 2 + xc]
                ).wait_recv()

    keys = n * rows
    chunk_blocks = min(n, 1024 // rows)
    chunk_keys = chunk_blocks * rows
    chunks = n // chunk_blocks
    scale = 1.0 / math.sqrt(head_dim)

    def tiles(s, c, j):
        part = bufs[s][pl.ds(c * chunk_blocks, chunk_blocks), pl.ds(j * rows, rows), :]
        return part.reshape(chunk_keys, LANES)

    def attend(s, q):
        def usable(c):
            at = pl.ds(c * chunk_blocks, chunk_blocks)
            flags = buf0[at, pl.ds(kv_tiles * rows, FLAG_ROWS), :].astype(jnp.float32)
            parts = []
            for g in range(chunk_blocks // per_tile):
                row = flags[g * per_tile, s : s + 1, :]
                for k in range(1, per_tile):
                    row = row + flags[g * per_tile + k, s : s + 1, :]
                parts.append(row)
            return jnp.concatenate(parts, axis=1) > 0.5

        def score(c):
            lhs = jnp.concatenate([tiles(s, c, j) for j in range(padded // LANES)], axis=1)
            return jnp.where(usable(c), dot_t(q, lhs) * scale, -1e30)

        def weigh(c, value, top):
            weight = jnp.where(usable(c), jnp.exp(value - top), 0.0)
            first = kv_tiles - padded // LANES
            rhs = jnp.concatenate([tiles(s, c, j) for j in range(first, kv_tiles)], axis=1)
            return jnp.sum(weight, -1, keepdims=True), dot(weight.astype(jnp.bfloat16), rhs)

        if chunks == 1:
            value = score(0)
            total, summed = weigh(0, value, jnp.max(value, -1, keepdims=True))
        else:

            def first_pass(c, top):
                value = score(c)
                scores[c] = value
                return jnp.maximum(top, jnp.max(value, -1, keepdims=True))

            top = lax.fori_loop(
                0, chunks, first_pass, jnp.full((heads * rows, 1), -1e30, jnp.float32)
            )

            def second_pass(c, state):
                total, summed = weigh(c, scores[c], top)
                return state[0] + total, state[1] + summed

            total, summed = lax.fori_loop(
                0,
                chunks,
                second_pass,
                (
                    jnp.zeros((heads * rows, 1), jnp.float32),
                    jnp.zeros((heads * rows, padded), jnp.float32),
                ),
            )
        inside = lax.broadcasted_iota(jnp.int32, (heads * rows, padded), 1) >= pad
        mixed = jnp.where(inside, summed / total, 0.0).astype(jnp.bfloat16)
        for h in range(heads):
            att[:, pl.ds(h * padded, padded)] = mixed[h * rows : (h + 1) * rows]

    def predict(hidden_rows):
        residual = hidden_rows.astype(jnp.float32) + dot(att[...], out_w[...])
        normed_out = normalize(residual, head_gain_ref[...])
        return softplus(dot(normed_out, head_w[...]) + bias_ref[...]).astype(jnp.bfloat16)

    wait_sibling(0)
    attend(0, q0)
    for load in loads[3:]:
        load.wait()
    fwd_pred[...] = predict(hid[0])
    swap.wait_recv()
    q1 = project_queries(normalize(partner_hid[...], gain))
    wait_sibling(1)
    attend(1, q1)
    rev_pred = predict(partner_hid[...])
    flip = jnp.where(
        lax.broadcasted_iota(jnp.int32, (rows, rows), 0)
        + lax.broadcasted_iota(jnp.int32, (rows, rows), 1)
        == rows - 1,
        1.0,
        0.0,
    ).astype(jnp.bfloat16)
    flipped = dot(flip, rev_pred).astype(jnp.bfloat16)
    result_ref[...] = 0.5 * (fwd_pred[...].astype(jnp.float32) + dot(flipped, perm_w[...]))

    swap.wait_send()
    for s in range(2):

        @pl.loop(0, line)
        def _(zc):
            pl.when(has_right & (zc <= z))(lambda: to_right(s, zc).wait_send())
            pl.when(has_left & (zc >= z))(lambda: to_left(s, zc).wait_send())
            to_across(s, zc).wait_send()
            for xc in range(2):
                to_sibling(s, zc, xc).wait_send()


def per_device(
    hidden,
    base_ids,
    attn_gain,
    q_weight,
    kv_weight,
    out_weight,
    head_gain,
    head_weight,
    head_bias,
    track_perm,
):
    n = lax.axis_size("tok")
    rows, width = hidden.shape[1], hidden.shape[2]
    head_dim = kv_weight.shape[1] // 2
    heads = q_weight.shape[1] // head_dim
    tracks = head_weight.shape[1]
    padded = -(-head_dim // LANES) * LANES
    line = n // 4
    kv_rows = kv_weight.shape[1] // LANES * rows
    chunk_blocks = min(n, 1024 // rows)
    chunks = n // chunk_blocks
    bf16 = jnp.bfloat16
    vmem = pl.BlockSpec(memory_space=pltpu.VMEM)
    hbm = pl.BlockSpec(memory_space=pl.ANY)
    score_shape = (chunks, heads * rows, chunk_blocks * rows) if chunks > 1 else (1, 8, LANES)
    return pl.pallas_call(
        functools.partial(kernel, n),
        out_shape=jax.ShapeDtypeStruct((rows, tracks), jnp.float32),
        in_specs=[hbm, vmem, vmem, hbm, hbm, hbm, vmem, hbm, vmem, vmem],
        out_specs=vmem,
        scratch_shapes=[
            pltpu.VMEM(hidden.shape, bf16),
            pltpu.VMEM((rows, width), bf16),
            pltpu.VMEM(kv_weight.shape, bf16),
            pltpu.VMEM(q_weight.shape, bf16),
            pltpu.VMEM((heads * padded, width), bf16),
            pltpu.VMEM(head_weight.shape, bf16),
            pltpu.VMEM((tracks, tracks), bf16),
            pltpu.VMEM((n, kv_rows + FLAG_ROWS, LANES), bf16),
            pltpu.VMEM((n, kv_rows, LANES), bf16),
            pltpu.VMEM(score_shape, jnp.float32),
            pltpu.VMEM((rows, heads * padded), bf16),
            pltpu.VMEM((rows, tracks), bf16),
            pltpu.SemaphoreType.DMA((4,)),
            pltpu.SemaphoreType.DMA((heads,)),
            pltpu.SemaphoreType.DMA((2,)),
            pltpu.SemaphoreType.DMA((2, n)),
            pltpu.SemaphoreType.DMA((2, line)),
            pltpu.SemaphoreType.DMA((2, line)),
            pltpu.SemaphoreType.DMA((2, line)),
            pltpu.SemaphoreType.DMA((2, 2 * line)),
        ],
        compiler_params=pltpu.CompilerParams(
            collective_id=0, has_side_effects=True, vmem_limit_bytes=60 * 1024 * 1024
        ),
    )(
        hidden,
        base_ids,
        attn_gain.reshape(1, -1),
        q_weight,
        kv_weight,
        out_weight,
        head_gain.reshape(1, -1),
        head_weight,
        head_bias.reshape(1, -1),
        track_perm.reshape(1, -1),
    )


def solution(mesh):
    placed = (P("grp", "tok", None), P("grp", "tok"), P(), P(), P(), P(), P(), P(), P(), P())
    return jax.shard_map(
        per_device, mesh=mesh, in_specs=placed, out_specs=P(("grp", "tok"), None), check_vma=False
    )
```

```python
import functools
import math

import jax
import jax.numpy as jnp
from jax import lax
from jax.experimental import pallas as pl
from jax.experimental.pallas import tpu as pltpu
from jax.sharding import PartitionSpec as P

MESH = pl.DeviceIdType.MESH
LANES = 128
FLAG_ROWS = 16


def normalize(rows, gain):
    widened = rows.astype(jnp.float32)
    mean = jnp.mean(widened * widened, -1, keepdims=True)
    return (widened * lax.rsqrt(mean + 1e-06) * gain.astype(jnp.float32)).astype(jnp.bfloat16)


def dot(a, b):
    return jnp.dot(a, b, preferred_element_type=jnp.float32)


def dot_t(a, b):
    return lax.dot_general(a, b, (((1,), (1,)), ((), ())), preferred_element_type=jnp.float32)


def softplus(v):
    return jnp.maximum(v, 0.0) + jnp.log1p(jnp.exp(-jnp.abs(v)))


def vector(ref):
    return ref[...].reshape(1, -1)


def kernel(
    n,
    hidden_ref,
    ids_ref,
    attn_gain_ref,
    q_hbm,
    kv_hbm,
    out_hbm,
    head_gain_ref,
    head_hbm,
    bias_ref,
    perm_ref,
    result_ref,
    hid,
    work,
    kv_w,
    q_w,
    out_w,
    head_w,
    perm_w,
    buf,
    stage,
    scores,
    att,
    final,
    other,
    load_sem,
    out_sem,
    swap_send,
    work_sem,
    pair_sem,
    final_sem,
    recv,
    send_l,
    send_r,
    send_x,
):
    line = n // 4
    rows, width = hid.shape[1], hid.shape[2]
    both = 2 * rows
    tracks = head_w.shape[1]
    head_dim = kv_w.shape[1] // 2
    heads = q_w.shape[1] // head_dim
    padded = att.shape[1] // heads
    pad = padded - head_dim
    kv_tiles = kv_w.shape[1] // LANES
    me = lax.axis_index("tok")
    core = lax.rem(me, 2)
    x = lax.rem(me // 2, 2)
    z = me // 4
    left, right = me - 4, me + 4
    across, sibling = me + 2 - 4 * x, me + 1 - 2 * core
    mirror_zero, mirror_one = n - 2 - me + core, n - 1 - me + core
    first = core == 0
    second = core == 1
    has_left, has_right = z > 0, z < line - 1

    def slot(zc, xc, cc):
        return (zc * 2 + xc) * 2 + cc

    def remote(src, dst, send_sem, recv_sem, device):
        return pltpu.make_async_remote_copy(
            src_ref=src,
            dst_ref=dst,
            send_sem=send_sem,
            recv_sem=recv_sem,
            device_id={"tok": device},
            device_id_type=MESH,
        )

    load_hid = pltpu.make_async_copy(hidden_ref, hid, load_sem.at[0])
    load_kv = pltpu.make_async_copy(kv_hbm, kv_w, load_sem.at[1])
    load_q = pltpu.make_async_copy(q_hbm, q_w, load_sem.at[2])
    load_head = pltpu.make_async_copy(head_hbm, head_w, load_sem.at[3])
    load_out = [
        pltpu.make_async_copy(
            out_hbm.at[pl.ds(h * head_dim, head_dim)],
            out_w.at[pl.ds(h * padded + pad, head_dim)],
            out_sem.at[h],
        )
        for h in range(heads)
    ]
    for load in [load_hid, load_kv, load_q] + load_out + [load_head]:
        load.start()

    barrier = pltpu.get_barrier_semaphore()

    def greet(device):
        pl.semaphore_signal(barrier, inc=1, device_id={"tok": device}, device_id_type=MESH)

    greet(sibling)
    greet(across)
    pl.when(has_left)(lambda: greet(left))
    pl.when(has_right)(lambda: greet(right))

    @pl.when(second)
    def _():
        greet(mirror_zero)
        greet(mirror_one)

    pl.semaphore_wait(barrier, 3 + has_left.astype(jnp.int32) + has_right.astype(jnp.int32))

    lower, upper = work.at[pl.ds(0, rows)], work.at[pl.ds(rows, rows)]
    keep_own = pltpu.make_async_copy(hidden_ref.at[0], lower, work_sem.at[0])
    give_pair = remote(hidden_ref.at[0], upper, swap_send.at[0], work_sem.at[1], sibling)
    swap_lower = remote(hidden_ref.at[1], lower, swap_send.at[1], work_sem.at[0], mirror_one)
    swap_upper = remote(hidden_ref.at[1], upper, swap_send.at[1], work_sem.at[1], mirror_one)

    @pl.when(first)
    def _():
        keep_own.start()
        swap_lower.start()

    @pl.when(second)
    def _():
        give_pair.start()
        swap_upper.start()

    def piece(index, device, send_sem):
        return remote(buf.at[index], buf.at[index], send_sem, recv.at[index], device)

    def to_left(zc, half):
        return piece(slot(zc, x, half), left, send_l.at[half, zc])

    def to_right(zc, half):
        return piece(slot(zc, x, half), right, send_r.at[half, zc])

    def to_across(zc, half):
        return piece(slot(zc, x, half), across, send_x.at[half, zc])

    pair = remote(stage, buf.at[me], pair_sem.at[0], recv.at[me], sibling)
    pair_in = remote(stage, buf.at[sibling], pair_sem.at[0], recv.at[sibling], sibling)

    load_hid.wait()
    gain = vector(attn_gain_ref)
    normed = normalize(hid[...].reshape(both, width), gain)
    load_kv.wait()
    key_value = dot(normed, kv_w[...])
    forward, reverse = key_value[:rows], key_value[rows:]
    mine = jnp.where(first, forward, reverse).astype(jnp.bfloat16)
    theirs = jnp.where(first, reverse, forward).astype(jnp.bfloat16)
    flag = jnp.where(ids_ref[...] != 4, 1.0, 0.0).astype(jnp.float32)
    per_tile = LANES // rows
    lane = lax.broadcasted_iota(jnp.int32, (1, LANES), 1)
    start = lax.rem(me, per_tile) * rows
    inside_tile = (lane >= start) & (lane < start + rows)

    def fill(block, values, flags):
        for j in range(kv_tiles):
            block[pl.ds(j * rows, rows), :] = values[:, j * LANES : (j + 1) * LANES]
        spread = jnp.where(inside_tile, jnp.concatenate([flags] * per_tile, axis=1), 0.0)
        spread = jnp.broadcast_to(spread, (FLAG_ROWS, LANES))
        block[pl.ds(kv_tiles * rows, FLAG_ROWS), :] = spread.astype(jnp.bfloat16)

    fill(stage, theirs, jnp.where(first, flag[1:2], flag[0:1]))
    pair.start()
    fill(buf.at[me], mine, jnp.where(first, flag[0:1], flag[1:2]))

    def spread_out(zc, half, go_left, go_right):
        if go_left:
            pl.when(has_left)(lambda: to_left(zc, half).start())
        if go_right:
            pl.when(has_right)(lambda: to_right(zc, half).start())
        to_across(zc, half).start()

    spread_out(z, core, True, True)
    pair_in.wait_recv()
    spread_out(z, 1 - core, True, True)

    def hop(d):
        for k in range(2):
            half = core if k == 0 else 1 - core

            @pl.when(z - d >= 0)
            def _():
                to_right(z - d, half).wait_recv()
                spread_out(z - d, half, False, True)

            @pl.when(z + d < line)
            def _():
                to_left(z + d, half).wait_recv()
                spread_out(z + d, half, True, False)

    def project_queries(normed_rows):
        q = dot(normed_rows, q_w[...])
        pieces = []
        inside = lax.broadcasted_iota(jnp.int32, (both, padded), 1) < head_dim
        for h in range(heads):
            base = h * head_dim // LANES * LANES
            shift = h * head_dim - base
            window = q[:, base : base + padded]
            if shift:
                window = pltpu.roll(window, padded - shift, axis=1)
            pieces.append(jnp.where(inside, window, 0.0).astype(jnp.bfloat16))
        return pieces

    perm_row = vector(perm_ref)

    def build_perm(i, _):
        step = perm_w.shape[0] // 4
        chunk = 128
        for k in range(step // chunk):
            base = i * step + k * chunk
            ids = lax.broadcasted_iota(jnp.int32, (chunk, tracks), 0) + base
            hit = jnp.where(ids == perm_row, 1.0, 0.0)
            perm_w[pl.ds(pl.multiple_of(base, chunk), chunk), :] = hit.astype(jnp.bfloat16)
        return 0

    out_zero = jnp.zeros((pad, width), jnp.bfloat16)
    for h in range(heads):
        out_w[pl.ds(h * padded, pad), :] = out_zero
    if line <= 4:
        for d in range(1, line):
            hop(d)
            if d < line - 1:
                build_perm(2 * d - 2, 0)
                build_perm(2 * d - 1, 0)
        for i in range(2 * max(line - 2, 0), 4):
            build_perm(i, 0)
    else:
        pl.loop(1, line)(hop)
        lax.fori_loop(0, 4, build_perm, 0)

    load_q.wait()
    pltpu.make_async_copy(hidden_ref.at[0], lower, work_sem.at[0]).wait()
    swap_upper.wait_recv()
    queries = project_queries(normalize(work[...], gain))

    @pl.loop(0, line)
    def _(zc):
        for half in range(2):
            piece(slot(zc, 1 - x, half), across, send_x.at[half, zc]).wait_recv()

    chunk_blocks = min(n, 1024 // rows)
    chunk_keys = chunk_blocks * rows
    chunks = n // chunk_blocks
    scale = 1.0 / math.sqrt(head_dim)

    def tiles(c, low, high):
        at = pl.ds(c * chunk_blocks, chunk_blocks)
        return jnp.concatenate(
            [
                buf[at, pl.ds(j * rows, rows), :].reshape(chunk_keys, LANES)
                for j in range(low, high)
            ],
            axis=1,
        )

    def usable(c):
        at = pl.ds(c * chunk_blocks, chunk_blocks)
        flags = buf[at, pl.ds(kv_tiles * rows, FLAG_ROWS), :].astype(jnp.float32)
        parts = []
        for g in range(chunk_blocks // per_tile):
            row = flags[g * per_tile, 0:1, :]
            for k in range(1, per_tile):
                row = row + flags[g * per_tile + k, 0:1, :]
            parts.append(row)
        return jnp.concatenate(parts, axis=1) > 0.5

    def score(c, q):
        return jnp.where(usable(c), dot_t(q, tiles(c, 0, padded // LANES)) * scale, -1e30)

    def weigh(c, value, top):
        weight = jnp.where(usable(c), jnp.exp(value - top), 0.0)
        rhs = tiles(c, kv_tiles - padded // LANES, kv_tiles)
        return jnp.sum(weight, -1, keepdims=True), dot(weight.astype(jnp.bfloat16), rhs)

    inside = lax.broadcasted_iota(jnp.int32, (both, padded), 1) >= pad
    for h in range(heads):
        if chunks == 1:
            value = score(0, queries[h])
            total, summed = weigh(0, value, jnp.max(value, -1, keepdims=True))
        else:

            def first_pass(c, top):
                value = score(c, queries[h])
                scores[c] = value
                return jnp.maximum(top, jnp.max(value, -1, keepdims=True))

            top = lax.fori_loop(
                0, chunks, first_pass, jnp.full((both, 1), -1e30, jnp.float32)
            )

            def second_pass(c, state):
                total, summed = weigh(c, scores[c], top)
                return state[0] + total, state[1] + summed

            empty = jnp.zeros((both, 1), jnp.float32), jnp.zeros((both, padded), jnp.float32)
            total, summed = lax.fori_loop(0, chunks, second_pass, empty)
        mixed = jnp.where(inside, summed / total, 0.0)
        att[:, pl.ds(h * padded, padded)] = mixed.astype(jnp.bfloat16)

    for load in load_out:
        load.wait()
    residual = work[...].astype(jnp.float32) + dot(att[...], out_w[...])
    normed_out = normalize(residual, vector(head_gain_ref))
    load_head.wait()
    pred = softplus(dot(normed_out, head_w[...]) + vector(bias_ref)).astype(jnp.bfloat16)

    @pl.when(first)
    def _():
        final[...] = pred

    @pl.when(second)
    def _():
        flip = jnp.where(
            lax.broadcasted_iota(jnp.int32, (both, both), 0)
            + lax.broadcasted_iota(jnp.int32, (both, both), 1)
            == both - 1,
            1.0,
            0.0,
        ).astype(jnp.bfloat16)
        flipped = dot(flip, pred).astype(jnp.bfloat16)
        final[...] = dot(flipped, perm_w[...]).astype(jnp.bfloat16)

    own = pl.ds(pl.multiple_of(core * rows, rows), rows)
    far = pl.ds(pl.multiple_of(rows - core * rows, rows), rows)
    exchange = remote(final.at[far], other, final_sem.at[0], final_sem.at[1], sibling)
    exchange.start()
    exchange.wait_recv()
    result_ref[...] = 0.5 * (final[own, :].astype(jnp.float32) + other[...].astype(jnp.float32))

    exchange.wait_send()
    pair.wait_send()
    swap_upper.wait_send()
    pl.when(second)(lambda: give_pair.wait_send())

    @pl.loop(0, line)
    def _(zc):
        for half in range(2):
            pl.when(has_right & (zc <= z))(lambda: to_right(zc, half).wait_send())
            pl.when(has_left & (zc >= z))(lambda: to_left(zc, half).wait_send())
            to_across(zc, half).wait_send()


def per_device(
    hidden,
    base_ids,
    attn_gain,
    q_weight,
    kv_weight,
    out_weight,
    head_gain,
    head_weight,
    head_bias,
    track_perm,
):
    n = lax.axis_size("tok")
    rows, width = hidden.shape[1], hidden.shape[2]
    head_dim = kv_weight.shape[1] // 2
    heads = q_weight.shape[1] // head_dim
    tracks = head_weight.shape[1]
    padded = -(-head_dim // LANES) * LANES
    line = n // 4
    kv_rows = kv_weight.shape[1] // LANES * rows
    chunk_blocks = min(n, 1024 // rows)
    chunks = n // chunk_blocks
    bf16 = jnp.bfloat16
    vmem = pl.BlockSpec(memory_space=pltpu.VMEM)
    hbm = pl.BlockSpec(memory_space=pl.ANY)
    score_shape = (chunks, 2 * rows, chunk_blocks * rows) if chunks > 1 else (1, 8, LANES)
    return pl.pallas_call(
        functools.partial(kernel, n),
        out_shape=jax.ShapeDtypeStruct((rows, tracks), jnp.float32),
        in_specs=[hbm, vmem, vmem, hbm, hbm, hbm, vmem, hbm, vmem, vmem],
        out_specs=vmem,
        scratch_shapes=[
            pltpu.VMEM(hidden.shape, bf16),
            pltpu.VMEM((2 * rows, width), bf16),
            pltpu.VMEM(kv_weight.shape, bf16),
            pltpu.VMEM(q_weight.shape, bf16),
            pltpu.VMEM((heads * padded, width), bf16),
            pltpu.VMEM(head_weight.shape, bf16),
            pltpu.VMEM((tracks, tracks), bf16),
            pltpu.VMEM((n, kv_rows + FLAG_ROWS, LANES), bf16),
            pltpu.VMEM((kv_rows + FLAG_ROWS, LANES), bf16),
            pltpu.VMEM(score_shape, jnp.float32),
            pltpu.VMEM((2 * rows, heads * padded), bf16),
            pltpu.VMEM((2 * rows, tracks), bf16),
            pltpu.VMEM((rows, tracks), bf16),
            pltpu.SemaphoreType.DMA((4,)),
            pltpu.SemaphoreType.DMA((heads,)),
            pltpu.SemaphoreType.DMA((2,)),
            pltpu.SemaphoreType.DMA((2,)),
            pltpu.SemaphoreType.DMA((1,)),
            pltpu.SemaphoreType.DMA((2,)),
            pltpu.SemaphoreType.DMA((n,)),
            pltpu.SemaphoreType.DMA((2, line)),
            pltpu.SemaphoreType.DMA((2, line)),
            pltpu.SemaphoreType.DMA((2, line)),
        ],
        compiler_params=pltpu.CompilerParams(
            collective_id=0, has_side_effects=True, vmem_limit_bytes=60 * 1024 * 1024
        ),
    )(
        hidden,
        base_ids,
        attn_gain,
        q_weight,
        kv_weight,
        out_weight,
        head_gain,
        head_weight,
        head_bias,
        track_perm,
    )


def solution(mesh):
    placed = (P("grp", "tok", None), P("grp", "tok"), P(), P(), P(), P(), P(), P(), P(), P())
    return jax.shard_map(
        per_device, mesh=mesh, in_specs=placed, out_specs=P(("grp", "tok"), None), check_vma=False
    )
```

```python
import functools
import math

import jax
import jax.numpy as jnp
from jax import lax
from jax.experimental import pallas as pl
from jax.experimental.pallas import tpu as pltpu
from jax.sharding import PartitionSpec as P

MESH = pl.DeviceIdType.MESH
LANES = 128
FLAG_ROWS = 16


def normalize(rows, gain):
    widened = rows.astype(jnp.float32)
    mean = jnp.mean(widened * widened, -1, keepdims=True)
    return (widened * lax.rsqrt(mean + 1e-06) * gain.astype(jnp.float32)).astype(jnp.bfloat16)


def dot(a, b):
    return jnp.dot(a, b, preferred_element_type=jnp.float32)


def dot_t(a, b):
    return lax.dot_general(a, b, (((1,), (1,)), ((), ())), preferred_element_type=jnp.float32)


def softplus(v):
    return jnp.maximum(v, 0.0) + jnp.log1p(jnp.exp(-jnp.abs(v)))


def vector(ref):
    return ref[...].reshape(1, -1)


def kernel(
    n,
    hidden_ref,
    ids_ref,
    attn_gain_ref,
    q_hbm,
    kv_hbm,
    out_hbm,
    head_gain_ref,
    head_hbm,
    bias_ref,
    perm_ref,
    result_ref,
    hid,
    work,
    kv_w,
    q_w,
    out_w,
    head_w,
    perm_w,
    buf,
    stage,
    scores,
    att,
    final,
    other,
    load_sem,
    out_sem,
    swap_send,
    work_sem,
    pair_sem,
    final_sem,
    recv,
    send_l,
    send_r,
    send_ll,
    send_rr,
    send_x,
):
    line = n // 4
    rows, width = hid.shape[1], hid.shape[2]
    both = 2 * rows
    tracks = head_w.shape[1]
    head_dim = kv_w.shape[1] // 2
    heads = q_w.shape[1] // head_dim
    padded = att.shape[1] // heads
    pad = padded - head_dim
    kv_tiles = kv_w.shape[1] // LANES
    me = lax.axis_index("tok")
    core = lax.rem(me, 2)
    x = lax.rem(me // 2, 2)
    z = me // 4
    left, right = me - 4, me + 4
    across, sibling = me + 2 - 4 * x, me + 1 - 2 * core
    mirror_zero, mirror_one = n - 2 - me + core, n - 1 - me + core
    first = core == 0
    second = core == 1
    has_left, has_right = z > 0, z < line - 1
    even = lax.rem(z, 2) == 0
    odd = lax.rem(z, 2) == 1
    skip_right, skip_left = even & (z < line - 2), odd & (z > 1)

    def slot(zc, xc, cc):
        return (zc * 2 + xc) * 2 + cc

    def remote(src, dst, send_sem, recv_sem, device):
        return pltpu.make_async_remote_copy(
            src_ref=src,
            dst_ref=dst,
            send_sem=send_sem,
            recv_sem=recv_sem,
            device_id={"tok": device},
            device_id_type=MESH,
        )

    load_hid = pltpu.make_async_copy(hidden_ref, hid, load_sem.at[0])
    load_kv = pltpu.make_async_copy(kv_hbm, kv_w, load_sem.at[1])
    load_q = pltpu.make_async_copy(q_hbm, q_w, load_sem.at[2])
    load_head = pltpu.make_async_copy(head_hbm, head_w, load_sem.at[3])
    load_out = [
        pltpu.make_async_copy(
            out_hbm.at[pl.ds(h * head_dim, head_dim)],
            out_w.at[pl.ds(h * padded + pad, head_dim)],
            out_sem.at[h],
        )
        for h in range(heads)
    ]
    for load in [load_hid, load_kv, load_q] + load_out + [load_head]:
        load.start()

    barrier = pltpu.get_barrier_semaphore()

    def greet(device):
        pl.semaphore_signal(barrier, inc=1, device_id={"tok": device}, device_id_type=MESH)

    greet(sibling)
    greet(across)
    pl.when(has_left)(lambda: greet(left))
    pl.when(has_right)(lambda: greet(right))
    pl.when(even & (z > 1))(lambda: greet(me - 8))
    pl.when(odd & (z < line - 2))(lambda: greet(me + 8))

    @pl.when(second)
    def _():
        greet(mirror_zero)
        greet(mirror_one)

    peers = [flag.astype(jnp.int32) for flag in (has_left, has_right, skip_left, skip_right)]
    pl.semaphore_wait(barrier, 3 + sum(peers))

    lower, upper = work.at[pl.ds(0, rows)], work.at[pl.ds(rows, rows)]
    keep_own = pltpu.make_async_copy(hidden_ref.at[0], lower, work_sem.at[0])
    give_pair = remote(hidden_ref.at[0], upper, swap_send.at[0], work_sem.at[1], sibling)
    swap_lower = remote(hidden_ref.at[1], lower, swap_send.at[1], work_sem.at[0], mirror_one)
    swap_upper = remote(hidden_ref.at[1], upper, swap_send.at[1], work_sem.at[1], mirror_one)

    @pl.when(first)
    def _():
        keep_own.start()
        swap_lower.start()

    @pl.when(second)
    def _():
        give_pair.start()
        swap_upper.start()

    def piece(index, device, send_sem):
        return remote(buf.at[index], buf.at[index], send_sem, recv.at[index], device)

    def to_left(zc, half):
        return piece(slot(zc, x, half), left, send_l.at[half, zc])

    def to_right(zc, half):
        return piece(slot(zc, x, half), right, send_r.at[half, zc])

    def to_left_two(zc, half):
        return piece(slot(zc, x, half), me - 8, send_ll.at[half, zc])

    def to_right_two(zc, half):
        return piece(slot(zc, x, half), me + 8, send_rr.at[half, zc])

    def to_across(zc, half):
        return piece(slot(zc, x, half), across, send_x.at[half, zc])

    pair = remote(stage, buf.at[me], pair_sem.at[0], recv.at[me], sibling)
    pair_in = remote(stage, buf.at[sibling], pair_sem.at[0], recv.at[sibling], sibling)

    out_zero = jnp.zeros((pad, width), jnp.bfloat16)
    for h in range(heads):
        out_w[pl.ds(h * padded, pad), :] = out_zero
    load_hid.wait()
    gain = vector(attn_gain_ref)
    normed = normalize(hid[...].reshape(both, width), gain)
    load_kv.wait()
    key_value = dot(normed, kv_w[...])
    forward, reverse = key_value[:rows], key_value[rows:]
    mine = jnp.where(first, forward, reverse).astype(jnp.bfloat16)
    theirs = jnp.where(first, reverse, forward).astype(jnp.bfloat16)
    flag = jnp.where(ids_ref[...] != 4, 1.0, 0.0).astype(jnp.float32)
    per_tile = LANES // rows
    lane = lax.broadcasted_iota(jnp.int32, (1, LANES), 1)
    start = lax.rem(me, per_tile) * rows
    inside_tile = (lane >= start) & (lane < start + rows)

    def fill(block, values, flags):
        for j in range(kv_tiles):
            block[pl.ds(j * rows, rows), :] = values[:, j * LANES : (j + 1) * LANES]
        spread = jnp.where(inside_tile, jnp.concatenate([flags] * per_tile, axis=1), 0.0)
        spread = jnp.broadcast_to(spread, (FLAG_ROWS, LANES))
        block[pl.ds(kv_tiles * rows, FLAG_ROWS), :] = spread.astype(jnp.bfloat16)

    fill(stage, theirs, jnp.where(first, flag[1:2], flag[0:1]))
    pair.start()
    fill(buf.at[me], mine, jnp.where(first, flag[0:1], flag[1:2]))

    def spread_out(zc, half, go_left, go_right):
        source = go_left and go_right
        if go_left:
            pl.when(skip_left)(lambda: to_left_two(zc, half).start())
            pl.when(has_left if source else has_left & odd)(
                lambda: to_left(zc, half).start()
            )
        if go_right:
            pl.when(skip_right)(lambda: to_right_two(zc, half).start())
            pl.when(has_right if source else has_right & even)(
                lambda: to_right(zc, half).start()
            )
        to_across(zc, half).start()

    spread_out(z, core, True, True)
    pair_in.wait_recv()
    spread_out(z, 1 - core, True, True)

    def hop(d):
        for k in range(2):
            half = core if k == 0 else 1 - core

            @pl.when(z - d >= 0)
            def _():
                to_right(z - d, half).wait_recv()
                spread_out(z - d, half, False, True)

            @pl.when(z + d < line)
            def _():
                to_left(z + d, half).wait_recv()
                spread_out(z + d, half, True, False)

    def project_queries(normed_rows):
        q = dot(normed_rows, q_w[...])
        pieces = []
        inside = lax.broadcasted_iota(jnp.int32, (both, padded), 1) < head_dim
        for h in range(heads):
            base = h * head_dim // LANES * LANES
            shift = h * head_dim - base
            window = q[:, base : base + padded]
            if shift:
                window = pltpu.roll(window, padded - shift, axis=1)
            pieces.append(jnp.where(inside, window, 0.0).astype(jnp.bfloat16))
        return pieces

    perm_row = vector(perm_ref)

    def build_perm(i, _):
        step = perm_w.shape[0] // 4
        chunk = 128
        for k in range(step // chunk):
            base = i * step + k * chunk
            ids = lax.broadcasted_iota(jnp.int32, (chunk, tracks), 0) + base
            hit = jnp.where(ids == perm_row, 1.0, 0.0)
            perm_w[pl.ds(pl.multiple_of(base, chunk), chunk), :] = hit.astype(jnp.bfloat16)
        return 0

    if line <= 4:
        for d in range(1, line):
            hop(d)
    else:
        pl.loop(1, line)(hop)

    @pl.when(second)
    def _():
        lax.fori_loop(0, 4, build_perm, 0)

    load_q.wait()
    pltpu.make_async_copy(hidden_ref.at[0], lower, work_sem.at[0]).wait()
    swap_upper.wait_recv()
    queries = project_queries(normalize(work[...], gain))

    @pl.loop(0, line)
    def _(zc):
        for half in range(2):
            piece(slot(zc, 1 - x, half), across, send_x.at[half, zc]).wait_recv()

    chunk_blocks = min(n, 1024 // rows)
    chunk_keys = chunk_blocks * rows
    chunks = n // chunk_blocks
    scale = 1.0 / math.sqrt(head_dim)

    def tiles(c, low, high):
        at = pl.ds(c * chunk_blocks, chunk_blocks)
        return jnp.concatenate(
            [
                buf[at, pl.ds(j * rows, rows), :].reshape(chunk_keys, LANES)
                for j in range(low, high)
            ],
            axis=1,
        )

    def usable(c):
        at = pl.ds(c * chunk_blocks, chunk_blocks)
        flags = buf[at, pl.ds(kv_tiles * rows, FLAG_ROWS), :].astype(jnp.float32)
        parts = []
        for g in range(chunk_blocks // per_tile):
            row = flags[g * per_tile, 0:1, :]
            for k in range(1, per_tile):
                row = row + flags[g * per_tile + k, 0:1, :]
            parts.append(row)
        return jnp.concatenate(parts, axis=1) > 0.5

    def score(c, q):
        return jnp.where(usable(c), dot_t(q, tiles(c, 0, padded // LANES)) * scale, -1e30)

    def weigh(c, value, top):
        weight = jnp.where(usable(c), jnp.exp(value - top), 0.0)
        rhs = tiles(c, kv_tiles - padded // LANES, kv_tiles)
        return jnp.sum(weight, -1, keepdims=True), dot(weight.astype(jnp.bfloat16), rhs)

    inside = lax.broadcasted_iota(jnp.int32, (both, padded), 1) >= pad
    for h in range(heads):
        if chunks == 1:
            value = score(0, queries[h])
            total, summed = weigh(0, value, jnp.max(value, -1, keepdims=True))
        else:

            def first_pass(c, top):
                value = score(c, queries[h])
                scores[c] = value
                return jnp.maximum(top, jnp.max(value, -1, keepdims=True))

            top = lax.fori_loop(
                0, chunks, first_pass, jnp.full((both, 1), -1e30, jnp.float32)
            )

            def second_pass(c, state):
                total, summed = weigh(c, scores[c], top)
                return state[0] + total, state[1] + summed

            empty = jnp.zeros((both, 1), jnp.float32), jnp.zeros((both, padded), jnp.float32)
            total, summed = lax.fori_loop(0, chunks, second_pass, empty)
        mixed = jnp.where(inside, summed / total, 0.0)
        att[:, pl.ds(h * padded, padded)] = mixed.astype(jnp.bfloat16)

    for load in load_out:
        load.wait()
    residual = work[...].astype(jnp.float32) + dot(att[...], out_w[...])
    normed_out = normalize(residual, vector(head_gain_ref))
    load_head.wait()
    pred = softplus(dot(normed_out, head_w[...]) + vector(bias_ref)).astype(jnp.bfloat16)

    @pl.when(first)
    def _():
        final[...] = pred

    @pl.when(second)
    def _():
        flip = jnp.where(
            lax.broadcasted_iota(jnp.int32, (both, both), 0)
            + lax.broadcasted_iota(jnp.int32, (both, both), 1)
            == both - 1,
            1.0,
            0.0,
        ).astype(jnp.bfloat16)
        flipped = dot(flip, pred).astype(jnp.bfloat16)
        final[...] = dot(flipped, perm_w[...]).astype(jnp.bfloat16)

    own = pl.ds(pl.multiple_of(core * rows, rows), rows)
    far = pl.ds(pl.multiple_of(rows - core * rows, rows), rows)
    exchange = remote(final.at[far], other, final_sem.at[0], final_sem.at[1], sibling)
    exchange.start()
    exchange.wait_recv()
    result_ref[...] = 0.5 * (final[own, :].astype(jnp.float32) + other[...].astype(jnp.float32))

    exchange.wait_send()
    pair.wait_send()
    swap_upper.wait_send()
    pl.when(second)(lambda: give_pair.wait_send())

    @pl.loop(0, line)
    def _(zc):
        for half in range(2):
            pl.when(has_right & ((zc == z) | (even & (zc < z))))(
                lambda: to_right(zc, half).wait_send()
            )
            pl.when(has_left & ((zc == z) | (odd & (zc > z))))(
                lambda: to_left(zc, half).wait_send()
            )
            pl.when(skip_right & (zc <= z))(lambda: to_right_two(zc, half).wait_send())
            pl.when(skip_left & (zc >= z))(lambda: to_left_two(zc, half).wait_send())
            to_across(zc, half).wait_send()


def per_device(
    hidden,
    base_ids,
    attn_gain,
    q_weight,
    kv_weight,
    out_weight,
    head_gain,
    head_weight,
    head_bias,
    track_perm,
):
    n = lax.axis_size("tok")
    rows, width = hidden.shape[1], hidden.shape[2]
    head_dim = kv_weight.shape[1] // 2
    heads = q_weight.shape[1] // head_dim
    tracks = head_weight.shape[1]
    padded = -(-head_dim // LANES) * LANES
    line = n // 4
    kv_rows = kv_weight.shape[1] // LANES * rows
    chunk_blocks = min(n, 1024 // rows)
    chunks = n // chunk_blocks
    bf16 = jnp.bfloat16
    vmem = pl.BlockSpec(memory_space=pltpu.VMEM)
    hbm = pl.BlockSpec(memory_space=pl.ANY)
    score_shape = (chunks, 2 * rows, chunk_blocks * rows) if chunks > 1 else (1, 8, LANES)
    return pl.pallas_call(
        functools.partial(kernel, n),
        out_shape=jax.ShapeDtypeStruct((rows, tracks), jnp.float32),
        in_specs=[hbm, vmem, vmem, hbm, hbm, hbm, vmem, hbm, vmem, vmem],
        out_specs=vmem,
        scratch_shapes=[
            pltpu.VMEM(hidden.shape, bf16),
            pltpu.VMEM((2 * rows, width), bf16),
            pltpu.VMEM(kv_weight.shape, bf16),
            pltpu.VMEM(q_weight.shape, bf16),
            pltpu.VMEM((heads * padded, width), bf16),
            pltpu.VMEM(head_weight.shape, bf16),
            pltpu.VMEM((tracks, tracks), bf16),
            pltpu.VMEM((n, kv_rows + FLAG_ROWS, LANES), bf16),
            pltpu.VMEM((kv_rows + FLAG_ROWS, LANES), bf16),
            pltpu.VMEM(score_shape, jnp.float32),
            pltpu.VMEM((2 * rows, heads * padded), bf16),
            pltpu.VMEM((2 * rows, tracks), bf16),
            pltpu.VMEM((rows, tracks), bf16),
            pltpu.SemaphoreType.DMA((4,)),
            pltpu.SemaphoreType.DMA((heads,)),
            pltpu.SemaphoreType.DMA((2,)),
            pltpu.SemaphoreType.DMA((2,)),
            pltpu.SemaphoreType.DMA((1,)),
            pltpu.SemaphoreType.DMA((2,)),
            pltpu.SemaphoreType.DMA((n,)),
            pltpu.SemaphoreType.DMA((2, line)),
            pltpu.SemaphoreType.DMA((2, line)),
            pltpu.SemaphoreType.DMA((2, line)),
            pltpu.SemaphoreType.DMA((2, line)),
            pltpu.SemaphoreType.DMA((2, line)),
        ],
        compiler_params=pltpu.CompilerParams(
            collective_id=0, has_side_effects=True, vmem_limit_bytes=60 * 1024 * 1024
        ),
    )(
        hidden,
        base_ids,
        attn_gain,
        q_weight,
        kv_weight,
        out_weight,
        head_gain,
        head_weight,
        head_bias,
        track_perm,
    )


def solution(mesh):
    placed = (P("grp", "tok", None), P("grp", "tok"), P(), P(), P(), P(), P(), P(), P(), P())
    return jax.shard_map(
        per_device, mesh=mesh, in_specs=placed, out_specs=P(("grp", "tok"), None), check_vma=False
    )
```

```python
import functools
import math

import jax
import jax.numpy as jnp
from jax import lax
from jax.experimental import pallas as pl
from jax.experimental.pallas import tpu as pltpu
from jax.sharding import PartitionSpec as P

MESH = pl.DeviceIdType.MESH
LANES = 128
FLAG_ROWS = 16


def normalize(rows, gain):
    widened = rows.astype(jnp.float32)
    mean = jnp.mean(widened * widened, -1, keepdims=True)
    return (widened * lax.rsqrt(mean + 1e-06) * gain.astype(jnp.float32)).astype(jnp.bfloat16)


def dot(a, b):
    return jnp.dot(a, b, preferred_element_type=jnp.float32)


def dot_t(a, b):
    return lax.dot_general(a, b, (((1,), (1,)), ((), ())), preferred_element_type=jnp.float32)


def softplus(v):
    return jnp.maximum(v, 0.0) + jnp.log(1.0 + jnp.exp(-jnp.abs(v)))


def vector(ref):
    return ref[...].reshape(1, -1)


def kernel(
    n,
    hidden_ref,
    ids_ref,
    attn_gain_ref,
    q_hbm,
    kv_hbm,
    out_hbm,
    head_gain_ref,
    head_hbm,
    bias_ref,
    perm_ref,
    result_ref,
    hid,
    work,
    kv_w,
    q_w,
    out_w,
    head_w,
    perm_w,
    buf,
    stage,
    att,
    final,
    other,
    load_sem,
    out_sem,
    swap_send,
    work_sem,
    pair_sem,
    final_sem,
    recv,
    send_l,
    send_r,
    send_ll,
    send_rr,
    send_x,
):
    line = n // 4
    rows, width = hid.shape[1], hid.shape[2]
    both = 2 * rows
    tracks = head_w.shape[1]
    head_dim = kv_w.shape[1] // 2
    heads = q_w.shape[1] // head_dim
    padded = att.shape[1] // heads
    pad = padded - head_dim
    kv_tiles = kv_w.shape[1] // LANES
    me = lax.axis_index("tok")
    core = lax.rem(me, 2)
    x = lax.rem(me // 2, 2)
    z = me // 4
    left, right = me - 4, me + 4
    across, sibling = me + 2 - 4 * x, me + 1 - 2 * core
    mirror_zero, mirror_one = n - 2 - me + core, n - 1 - me + core
    first = core == 0
    second = core == 1
    has_left, has_right = z > 0, z < line - 1
    even = lax.rem(z, 2) == 0
    odd = lax.rem(z, 2) == 1
    skip_right, skip_left = even & (z < line - 2), odd & (z > 1)

    def slot(zc, xc, cc):
        return (xc * line + zc) * 2 + cc

    mine_at, pair_at = slot(z, x, core), slot(z, x, 1 - core)

    def remote(src, dst, send_sem, recv_sem, device):
        return pltpu.make_async_remote_copy(
            src_ref=src,
            dst_ref=dst,
            send_sem=send_sem,
            recv_sem=recv_sem,
            device_id={"tok": device},
            device_id_type=MESH,
        )

    load_hid = pltpu.make_async_copy(hidden_ref, hid, load_sem.at[0])
    load_kv = pltpu.make_async_copy(kv_hbm, kv_w, load_sem.at[1])
    load_q = pltpu.make_async_copy(q_hbm, q_w, load_sem.at[2])
    load_head = pltpu.make_async_copy(head_hbm, head_w, load_sem.at[3])
    load_out = [
        pltpu.make_async_copy(
            out_hbm.at[pl.ds(h * head_dim, head_dim)],
            out_w.at[pl.ds(h * padded + pad, head_dim)],
            out_sem.at[h],
        )
        for h in range(heads)
    ]
    for load in [load_hid, load_kv, load_q] + load_out + [load_head]:
        load.start()

    barrier = pltpu.get_barrier_semaphore()

    def greet(device):
        pl.semaphore_signal(barrier, inc=1, device_id={"tok": device}, device_id_type=MESH)

    greet(sibling)
    greet(across)
    pl.when(has_left)(lambda: greet(left))
    pl.when(has_right)(lambda: greet(right))
    pl.when(even & (z > 1))(lambda: greet(me - 8))
    pl.when(odd & (z < line - 2))(lambda: greet(me + 8))

    @pl.when(second)
    def _():
        greet(mirror_zero)
        greet(mirror_one)

    peers = [flag.astype(jnp.int32) for flag in (has_left, has_right, skip_left, skip_right)]
    pl.semaphore_wait(barrier, 3 + sum(peers))

    lower, upper = work.at[pl.ds(0, rows)], work.at[pl.ds(rows, rows)]
    keep_own = pltpu.make_async_copy(hidden_ref.at[0], lower, work_sem.at[0])
    give_pair = remote(hidden_ref.at[0], upper, swap_send.at[0], work_sem.at[1], sibling)
    swap_lower = remote(hidden_ref.at[1], lower, swap_send.at[1], work_sem.at[0], mirror_one)
    swap_upper = remote(hidden_ref.at[1], upper, swap_send.at[1], work_sem.at[1], mirror_one)

    @pl.when(first)
    def _():
        keep_own.start()
        swap_lower.start()

    @pl.when(second)
    def _():
        give_pair.start()
        swap_upper.start()

    def piece(index, device, send_sem):
        return remote(buf.at[index], buf.at[index], send_sem, recv.at[index], device)

    def to_left(zc, half):
        return piece(slot(zc, x, half), left, send_l.at[half, zc])

    def to_right(zc, half):
        return piece(slot(zc, x, half), right, send_r.at[half, zc])

    def to_left_two(zc, half):
        return piece(slot(zc, x, half), me - 8, send_ll.at[half, zc])

    def to_right_two(zc, half):
        return piece(slot(zc, x, half), me + 8, send_rr.at[half, zc])

    def to_across(zc, half):
        return piece(slot(zc, x, half), across, send_x.at[half, zc])

    pair = remote(stage, buf.at[mine_at], pair_sem.at[0], recv.at[mine_at], sibling)
    pair_in = remote(stage, buf.at[pair_at], pair_sem.at[0], recv.at[pair_at], sibling)

    out_zero = jnp.zeros((pad, width), jnp.bfloat16)
    for h in range(heads):
        out_w[pl.ds(h * padded, pad), :] = out_zero
    load_hid.wait()
    gain = vector(attn_gain_ref)
    normed = normalize(hid[...].reshape(both, width), gain)
    load_kv.wait()
    key_value = dot(normed, kv_w[...])
    forward, reverse = key_value[:rows], key_value[rows:]
    mine = jnp.where(first, forward, reverse).astype(jnp.bfloat16)
    theirs = jnp.where(first, reverse, forward).astype(jnp.bfloat16)
    flag = jnp.where(ids_ref[...] != 4, 1.0, 0.0).astype(jnp.float32)
    per_tile = LANES // rows
    lane = lax.broadcasted_iota(jnp.int32, (1, LANES), 1)
    start = lax.rem(mine_at, per_tile) * rows
    inside_tile = (lane >= start) & (lane < start + rows)

    def fill(block, values, flags):
        for j in range(kv_tiles):
            block[pl.ds(j * rows, rows), :] = values[:, j * LANES : (j + 1) * LANES]
        spread = jnp.where(inside_tile, jnp.concatenate([flags] * per_tile, axis=1), 0.0)
        spread = jnp.broadcast_to(spread, (FLAG_ROWS, LANES))
        block[pl.ds(kv_tiles * rows, FLAG_ROWS), :] = spread.astype(jnp.bfloat16)

    fill(stage, theirs, jnp.where(first, flag[1:2], flag[0:1]))
    pair.start()
    fill(buf.at[mine_at], mine, jnp.where(first, flag[0:1], flag[1:2]))

    def spread_out(zc, half, go_left, go_right):
        source = go_left and go_right
        if go_left:
            pl.when(skip_left)(lambda: to_left_two(zc, half).start())
            pl.when(has_left if source else has_left & odd)(
                lambda: to_left(zc, half).start()
            )
        if go_right:
            pl.when(skip_right)(lambda: to_right_two(zc, half).start())
            pl.when(has_right if source else has_right & even)(
                lambda: to_right(zc, half).start()
            )
        to_across(zc, half).start()

    spread_out(z, core, True, True)
    pair_in.wait_recv()
    spread_out(z, 1 - core, True, True)

    def hop(d):
        for k in range(2):
            half = core if k == 0 else 1 - core

            @pl.when(z - d >= 0)
            def _():
                to_right(z - d, half).wait_recv()
                spread_out(z - d, half, False, True)

            @pl.when(z + d < line)
            def _():
                to_left(z + d, half).wait_recv()
                spread_out(z + d, half, True, False)

    def project_queries(normed_rows):
        q = dot(normed_rows, q_w[...])
        pieces = []
        inside = lax.broadcasted_iota(jnp.int32, (both, padded), 1) < head_dim
        for h in range(heads):
            base = h * head_dim // LANES * LANES
            shift = h * head_dim - base
            window = q[:, base : base + padded]
            if shift:
                window = pltpu.roll(window, padded - shift, axis=1)
            pieces.append(jnp.where(inside, window, 0.0).astype(jnp.bfloat16))
        return pieces

    perm_row = vector(perm_ref)

    def build_perm(i, _):
        step = perm_w.shape[0] // 4
        chunk = 128
        for k in range(step // chunk):
            base = i * step + k * chunk
            ids = lax.broadcasted_iota(jnp.int32, (chunk, tracks), 0) + base
            hit = jnp.where(ids == perm_row, 1.0, 0.0)
            perm_w[pl.ds(pl.multiple_of(base, chunk), chunk), :] = hit.astype(jnp.bfloat16)
        return 0

    def make_queries():
        load_q.wait()
        pltpu.make_async_copy(hidden_ref.at[0], lower, work_sem.at[0]).wait()
        swap_upper.wait_recv()
        return project_queries(normalize(work[...], gain))

    if line <= 4:
        for d in range(1, line):
            hop(d)
            if d == 1:
                build_perm(0, 0)
                build_perm(1, 0)
            if d == line - 2:
                build_perm(2, 0)
                build_perm(3, 0)
                queries = make_queries()
    else:
        pl.loop(1, line)(hop)
    if not 3 <= line <= 4:
        lax.fori_loop(0, 4, build_perm, 0)
        queries = make_queries()

    blocks = 2 * line
    keys = blocks * rows
    scale = 1.0 / math.sqrt(head_dim)

    def part(column):
        at = pl.ds(column * blocks, blocks)

        def tiles(low, high):
            parts = [
                buf[at, pl.ds(j * rows, rows), :].reshape(keys, LANES) for j in range(low, high)
            ]
            return jnp.concatenate(parts, axis=1)

        flags = buf[at, pl.ds(kv_tiles * rows, FLAG_ROWS), :].astype(jnp.float32)
        parts = []
        for g in range(blocks // per_tile):
            row = flags[g * per_tile, 0:1, :]
            for k in range(1, per_tile):
                row = row + flags[g * per_tile + k, 0:1, :]
            parts.append(row)
        usable = jnp.concatenate(parts, axis=1) > 0.5
        lhs = tiles(0, padded // LANES)
        rhs = tiles(kv_tiles - padded // LANES, kv_tiles)
        states = []
        for h in range(heads):
            value = jnp.where(usable, dot_t(queries[h], lhs) * scale, -1e30)
            top = jnp.max(value, -1, keepdims=True)
            weight = jnp.where(usable, jnp.exp(value - top), 0.0)
            total = jnp.sum(weight, -1, keepdims=True)
            states.append((top, total, dot(weight.astype(jnp.bfloat16), rhs)))
        return states

    near = part(x)

    @pl.loop(0, line)
    def _(zc):
        for half in range(2):
            piece(slot(zc, 1 - x, half), across, send_x.at[half, zc]).wait_recv()

    distant = part(1 - x)
    inside = lax.broadcasted_iota(jnp.int32, (both, padded), 1) >= pad
    for h in range(heads):
        (top_a, total_a, sum_a), (top_b, total_b, sum_b) = near[h], distant[h]
        top = jnp.maximum(top_a, top_b)
        scale_a, scale_b = jnp.exp(top_a - top), jnp.exp(top_b - top)
        total = total_a * scale_a + total_b * scale_b
        mixed = (sum_a * scale_a + sum_b * scale_b) / total
        att[:, pl.ds(h * padded, padded)] = jnp.where(inside, mixed, 0.0).astype(jnp.bfloat16)

    for load in load_out:
        load.wait()
    residual = work[...].astype(jnp.float32) + dot(att[...], out_w[...])
    normed_out = normalize(residual, vector(head_gain_ref))
    load_head.wait()
    pred = softplus(dot(normed_out, head_w[...]) + vector(bias_ref)).astype(jnp.bfloat16)

    @pl.when(first)
    def _():
        final[...] = pred

    @pl.when(second)
    def _():
        flip = jnp.where(
            lax.broadcasted_iota(jnp.int32, (both, both), 0)
            + lax.broadcasted_iota(jnp.int32, (both, both), 1)
            == both - 1,
            1.0,
            0.0,
        ).astype(jnp.bfloat16)
        flipped = dot(flip, pred).astype(jnp.bfloat16)
        final[...] = flipped

    own = pl.ds(pl.multiple_of(core * rows, rows), rows)
    far = pl.ds(pl.multiple_of(rows - core * rows, rows), rows)
    exchange = remote(final.at[far], other, final_sem.at[0], final_sem.at[1], sibling)
    exchange.start()

    @pl.when(first)
    def _():
        exchange.wait_recv()
        result_ref[...] = 0.5 * (
            final[own, :].astype(jnp.float32) + dot(other[...], perm_w[...])
        )

    @pl.when(second)
    def _():
        turned = dot(final[own, :], perm_w[...])
        exchange.wait_recv()
        result_ref[...] = 0.5 * (other[...].astype(jnp.float32) + turned)

    exchange.wait_send()
    pair.wait_send()
    swap_upper.wait_send()
    pl.when(second)(lambda: give_pair.wait_send())

    @pl.loop(0, line)
    def _(zc):
        for half in range(2):
            pl.when(has_right & ((zc == z) | (even & (zc < z))))(
                lambda: to_right(zc, half).wait_send()
            )
            pl.when(has_left & ((zc == z) | (odd & (zc > z))))(
                lambda: to_left(zc, half).wait_send()
            )
            pl.when(skip_right & (zc <= z))(lambda: to_right_two(zc, half).wait_send())
            pl.when(skip_left & (zc >= z))(lambda: to_left_two(zc, half).wait_send())
            to_across(zc, half).wait_send()


def per_device(
    hidden,
    base_ids,
    attn_gain,
    q_weight,
    kv_weight,
    out_weight,
    head_gain,
    head_weight,
    head_bias,
    track_perm,
):
    n = lax.axis_size("tok")
    rows, width = hidden.shape[1], hidden.shape[2]
    head_dim = kv_weight.shape[1] // 2
    heads = q_weight.shape[1] // head_dim
    tracks = head_weight.shape[1]
    padded = -(-head_dim // LANES) * LANES
    line = n // 4
    kv_rows = kv_weight.shape[1] // LANES * rows
    bf16 = jnp.bfloat16
    vmem = pl.BlockSpec(memory_space=pltpu.VMEM)
    hbm = pl.BlockSpec(memory_space=pl.ANY)
    return pl.pallas_call(
        functools.partial(kernel, n),
        out_shape=jax.ShapeDtypeStruct((rows, tracks), jnp.float32),
        in_specs=[hbm, vmem, vmem, hbm, hbm, hbm, vmem, hbm, vmem, vmem],
        out_specs=vmem,
        scratch_shapes=[
            pltpu.VMEM(hidden.shape, bf16),
            pltpu.VMEM((2 * rows, width), bf16),
            pltpu.VMEM(kv_weight.shape, bf16),
            pltpu.VMEM(q_weight.shape, bf16),
            pltpu.VMEM((heads * padded, width), bf16),
            pltpu.VMEM(head_weight.shape, bf16),
            pltpu.VMEM((tracks, tracks), bf16),
            pltpu.VMEM((n, kv_rows + FLAG_ROWS, LANES), bf16),
            pltpu.VMEM((kv_rows + FLAG_ROWS, LANES), bf16),
            pltpu.VMEM((2 * rows, heads * padded), bf16),
            pltpu.VMEM((2 * rows, tracks), bf16),
            pltpu.VMEM((rows, tracks), bf16),
            pltpu.SemaphoreType.DMA((4,)),
            pltpu.SemaphoreType.DMA((heads,)),
            pltpu.SemaphoreType.DMA((2,)),
            pltpu.SemaphoreType.DMA((2,)),
            pltpu.SemaphoreType.DMA((1,)),
            pltpu.SemaphoreType.DMA((2,)),
            pltpu.SemaphoreType.DMA((n,)),
            pltpu.SemaphoreType.DMA((2, line)),
            pltpu.SemaphoreType.DMA((2, line)),
            pltpu.SemaphoreType.DMA((2, line)),
            pltpu.SemaphoreType.DMA((2, line)),
            pltpu.SemaphoreType.DMA((2, line)),
        ],
        compiler_params=pltpu.CompilerParams(
            collective_id=0, has_side_effects=True, vmem_limit_bytes=60 * 1024 * 1024
        ),
    )(
        hidden,
        base_ids,
        attn_gain,
        q_weight,
        kv_weight,
        out_weight,
        head_gain,
        head_weight,
        head_bias,
        track_perm,
    )


def solution(mesh):
    placed = (P("grp", "tok", None), P("grp", "tok"), P(), P(), P(), P(), P(), P(), P(), P())
    return jax.shard_map(
        per_device, mesh=mesh, in_specs=placed, out_specs=P(("grp", "tok"), None), check_vma=False
    )
```

```python
import functools
import math

import jax
import jax.numpy as jnp
from jax import lax
from jax.experimental import pallas as pl
from jax.experimental.pallas import tpu as pltpu
from jax.sharding import PartitionSpec as P

MESH = pl.DeviceIdType.MESH
LANES = 128
FLAG_ROWS = 16


def normalize(rows, gain):
    widened = rows.astype(jnp.float32)
    mean = jnp.mean(widened * widened, -1, keepdims=True)
    return (widened * lax.rsqrt(mean + 1e-06) * gain.astype(jnp.float32)).astype(jnp.bfloat16)


def dot(a, b):
    return jnp.dot(a, b, preferred_element_type=jnp.float32)


def dot_t(a, b):
    return lax.dot_general(a, b, (((1,), (1,)), ((), ())), preferred_element_type=jnp.float32)


def softplus(v):
    return jnp.maximum(v, 0.0) + jnp.log(1.0 + jnp.exp(-jnp.abs(v)))


def vector(ref):
    return ref[...].reshape(1, -1)


def kernel(
    n,
    hidden_ref,
    ids_ref,
    attn_gain_ref,
    q_hbm,
    kv_hbm,
    out_hbm,
    head_gain_ref,
    head_hbm,
    bias_ref,
    perm_ref,
    result_ref,
    hid,
    work,
    kv_w,
    q_w,
    out_w,
    head_w,
    perm_w,
    buf,
    stage,
    att,
    final,
    other,
    load_sem,
    out_sem,
    swap_send,
    work_sem,
    pair_sem,
    final_sem,
    recv,
    send_l,
    send_r,
    send_x,
):
    line = n // 4
    rows, width = hid.shape[1], hid.shape[2]
    both = 2 * rows
    tracks = head_w.shape[1]
    head_dim = kv_w.shape[1] // 2
    heads = q_w.shape[1] // head_dim
    padded = att.shape[1] // heads
    pad = padded - head_dim
    kv_tiles = kv_w.shape[1] // LANES
    me = lax.axis_index("tok")
    core = lax.rem(me, 2)
    x = lax.rem(me // 2, 2)
    z = me // 4
    left, right = me - 4, me + 4
    across, sibling = me + 2 - 4 * x, me + 1 - 2 * core
    mirror_zero, mirror_one = n - 2 - me + core, n - 1 - me + core
    first = core == 0
    second = core == 1
    has_left, has_right = z > 0, z < line - 1

    def slot(zc, xc, cc):
        return (xc * line + zc) * 2 + cc

    mine_at, pair_at = slot(z, x, core), slot(z, x, 1 - core)

    def remote(src, dst, send_sem, recv_sem, device):
        return pltpu.make_async_remote_copy(
            src_ref=src,
            dst_ref=dst,
            send_sem=send_sem,
            recv_sem=recv_sem,
            device_id={"tok": device},
            device_id_type=MESH,
        )

    load_hid = pltpu.make_async_copy(hidden_ref, hid, load_sem.at[0])
    load_kv = pltpu.make_async_copy(kv_hbm, kv_w, load_sem.at[1])
    load_q = pltpu.make_async_copy(q_hbm, q_w, load_sem.at[2])
    load_head = pltpu.make_async_copy(head_hbm, head_w, load_sem.at[3])
    load_out = [
        pltpu.make_async_copy(
            out_hbm.at[pl.ds(h * head_dim, head_dim)],
            out_w.at[pl.ds(h * padded + pad, head_dim)],
            out_sem.at[h],
        )
        for h in range(heads)
    ]
    for load in [load_hid, load_kv, load_q] + load_out + [load_head]:
        load.start()

    barrier = pltpu.get_barrier_semaphore()

    def greet(device):
        pl.semaphore_signal(barrier, inc=1, device_id={"tok": device}, device_id_type=MESH)

    greet(sibling)
    greet(across)
    pl.when(has_left)(lambda: greet(left))
    pl.when(has_right)(lambda: greet(right))

    @pl.when(second)
    def _():
        greet(mirror_zero)
        greet(mirror_one)

    peers = [flag.astype(jnp.int32) for flag in (has_left, has_right)]
    pl.semaphore_wait(barrier, 3 + sum(peers))

    lower, upper = work.at[pl.ds(0, rows)], work.at[pl.ds(rows, rows)]
    keep_own = pltpu.make_async_copy(hidden_ref.at[0], lower, work_sem.at[0])
    give_pair = remote(hidden_ref.at[0], upper, swap_send.at[0], work_sem.at[1], sibling)
    swap_lower = remote(hidden_ref.at[1], lower, swap_send.at[1], work_sem.at[0], mirror_one)
    swap_upper = remote(hidden_ref.at[1], upper, swap_send.at[1], work_sem.at[1], mirror_one)

    @pl.when(first)
    def _():
        keep_own.start()
        swap_lower.start()

    @pl.when(second)
    def _():
        give_pair.start()
        swap_upper.start()

    def piece(index, device, send_sem):
        return remote(buf.at[index], buf.at[index], send_sem, recv.at[index], device)

    def to_left(zc, half):
        return piece(slot(zc, x, half), left, send_l.at[half, zc])

    def to_right(zc, half):
        return piece(slot(zc, x, half), right, send_r.at[half, zc])

    def to_across(zc, half):
        return piece(slot(zc, x, half), across, send_x.at[half, zc])

    pair = remote(stage, buf.at[mine_at], pair_sem.at[0], recv.at[mine_at], sibling)
    pair_in = remote(stage, buf.at[pair_at], pair_sem.at[0], recv.at[pair_at], sibling)

    out_zero = jnp.zeros((pad, width), jnp.bfloat16)
    for h in range(heads):
        out_w[pl.ds(h * padded, pad), :] = out_zero
    load_hid.wait()
    gain = vector(attn_gain_ref)
    normed = normalize(hid[...].reshape(both, width), gain)
    load_kv.wait()
    key_value = dot(normed, kv_w[...])
    forward, reverse = key_value[:rows], key_value[rows:]
    mine = jnp.where(first, forward, reverse).astype(jnp.bfloat16)
    theirs = jnp.where(first, reverse, forward).astype(jnp.bfloat16)
    flag = jnp.where(ids_ref[...] != 4, 1.0, 0.0).astype(jnp.float32)
    per_tile = LANES // rows
    lane = lax.broadcasted_iota(jnp.int32, (1, LANES), 1)
    start = lax.rem(mine_at, per_tile) * rows
    inside_tile = (lane >= start) & (lane < start + rows)

    def fill(block, values, flags):
        for j in range(kv_tiles):
            block[pl.ds(j * rows, rows), :] = values[:, j * LANES : (j + 1) * LANES]
        spread = jnp.where(inside_tile, jnp.concatenate([flags] * per_tile, axis=1), 0.0)
        spread = jnp.broadcast_to(spread, (FLAG_ROWS, LANES))
        block[pl.ds(kv_tiles * rows, FLAG_ROWS), :] = spread.astype(jnp.bfloat16)

    fill(stage, theirs, jnp.where(first, flag[1:2], flag[0:1]))
    pair.start()
    fill(buf.at[mine_at], mine, jnp.where(first, flag[0:1], flag[1:2]))

    def spread_out(zc, half, go_left, go_right):
        if go_left:
            pl.when(has_left)(lambda: to_left(zc, half).start())
        if go_right:
            pl.when(has_right)(lambda: to_right(zc, half).start())
        to_across(zc, half).start()

    spread_out(z, core, True, True)
    pair_in.wait_recv()
    spread_out(z, 1 - core, True, True)

    def hop(d):
        for k in range(2):
            half = core if k == 0 else 1 - core

            @pl.when(z - d >= 0)
            def _():
                to_right(z - d, half).wait_recv()
                spread_out(z - d, half, False, True)

            @pl.when(z + d < line)
            def _():
                to_left(z + d, half).wait_recv()
                spread_out(z + d, half, True, False)

    def project_queries(normed_rows):
        q = dot(normed_rows, q_w[...])
        pieces = []
        inside = lax.broadcasted_iota(jnp.int32, (both, padded), 1) < head_dim
        for h in range(heads):
            base = h * head_dim // LANES * LANES
            shift = h * head_dim - base
            window = q[:, base : base + padded]
            if shift:
                window = pltpu.roll(window, padded - shift, axis=1)
            pieces.append(jnp.where(inside, window, 0.0).astype(jnp.bfloat16))
        return pieces

    perm_row = vector(perm_ref)

    def build_perm(i, _):
        step = perm_w.shape[0] // 4
        chunk = 128
        for k in range(step // chunk):
            base = i * step + k * chunk
            ids = lax.broadcasted_iota(jnp.int32, (chunk, tracks), 0) + base
            hit = jnp.where(ids == perm_row, 1.0, 0.0)
            perm_w[pl.ds(pl.multiple_of(base, chunk), chunk), :] = hit.astype(jnp.bfloat16)
        return 0

    def make_queries():
        load_q.wait()
        pltpu.make_async_copy(hidden_ref.at[0], lower, work_sem.at[0]).wait()
        swap_upper.wait_recv()
        return project_queries(normalize(work[...], gain))

    if line <= 4:
        for d in range(1, line):
            hop(d)
            if d == 1:
                build_perm(0, 0)
                build_perm(1, 0)
            if d == line - 2:
                build_perm(2, 0)
                build_perm(3, 0)
    else:
        pl.loop(1, line)(hop)
    if not 3 <= line <= 4:
        lax.fori_loop(0, 4, build_perm, 0)
    queries = make_queries()

    blocks = 2 * line
    keys = blocks * rows
    scale = 1.0 / math.sqrt(head_dim)

    def part(column):
        at = pl.ds(column * blocks, blocks)

        def tiles(low, high):
            parts = [
                buf[at, pl.ds(j * rows, rows), :].reshape(keys, LANES) for j in range(low, high)
            ]
            return jnp.concatenate(parts, axis=1)

        flags = buf[at, pl.ds(kv_tiles * rows, FLAG_ROWS), :].astype(jnp.float32)
        parts = []
        for g in range(blocks // per_tile):
            row = flags[g * per_tile, 0:1, :]
            for k in range(1, per_tile):
                row = row + flags[g * per_tile + k, 0:1, :]
            parts.append(row)
        usable = jnp.concatenate(parts, axis=1) > 0.5
        lhs = tiles(0, padded // LANES)
        rhs = tiles(kv_tiles - padded // LANES, kv_tiles)
        states = []
        for h in range(heads):
            value = jnp.where(usable, dot_t(queries[h], lhs) * scale, -1e30)
            top = jnp.max(value, -1, keepdims=True)
            weight = jnp.where(usable, jnp.exp(value - top), 0.0)
            total = jnp.sum(weight, -1, keepdims=True)
            states.append((top, total, dot(weight.astype(jnp.bfloat16), rhs)))
        return states

    near = part(x)

    @pl.loop(0, line)
    def _(zc):
        for half in range(2):
            piece(slot(zc, 1 - x, half), across, send_x.at[half, zc]).wait_recv()

    distant = part(1 - x)
    inside = lax.broadcasted_iota(jnp.int32, (both, padded), 1) >= pad
    for h in range(heads):
        (top_a, total_a, sum_a), (top_b, total_b, sum_b) = near[h], distant[h]
        top = jnp.maximum(top_a, top_b)
        scale_a, scale_b = jnp.exp(top_a - top), jnp.exp(top_b - top)
        total = total_a * scale_a + total_b * scale_b
        mixed = (sum_a * scale_a + sum_b * scale_b) / total
        att[:, pl.ds(h * padded, padded)] = jnp.where(inside, mixed, 0.0).astype(jnp.bfloat16)

    for load in load_out:
        load.wait()
    residual = work[...].astype(jnp.float32) + dot(att[...], out_w[...])
    normed_out = normalize(residual, vector(head_gain_ref))
    load_head.wait()
    pred = softplus(dot(normed_out, head_w[...]) + vector(bias_ref)).astype(jnp.bfloat16)

    @pl.when(first)
    def _():
        final[...] = pred

    @pl.when(second)
    def _():
        flip = jnp.where(
            lax.broadcasted_iota(jnp.int32, (both, both), 0)
            + lax.broadcasted_iota(jnp.int32, (both, both), 1)
            == both - 1,
            1.0,
            0.0,
        ).astype(jnp.bfloat16)
        flipped = dot(flip, pred).astype(jnp.bfloat16)
        final[...] = flipped

    own = pl.ds(pl.multiple_of(core * rows, rows), rows)
    far = pl.ds(pl.multiple_of(rows - core * rows, rows), rows)
    exchange = remote(final.at[far], other, final_sem.at[0], final_sem.at[1], sibling)
    exchange.start()

    @pl.when(first)
    def _():
        exchange.wait_recv()
        result_ref[...] = 0.5 * (
            final[own, :].astype(jnp.float32) + dot(other[...], perm_w[...])
        )

    @pl.when(second)
    def _():
        turned = dot(final[own, :], perm_w[...])
        exchange.wait_recv()
        result_ref[...] = 0.5 * (other[...].astype(jnp.float32) + turned)

    exchange.wait_send()
    pair.wait_send()
    swap_upper.wait_send()
    pl.when(second)(lambda: give_pair.wait_send())

    @pl.loop(0, line)
    def _(zc):
        for half in range(2):
            pl.when(has_right & (zc <= z))(lambda: to_right(zc, half).wait_send())
            pl.when(has_left & (zc >= z))(lambda: to_left(zc, half).wait_send())
            to_across(zc, half).wait_send()


def per_device(
    hidden,
    base_ids,
    attn_gain,
    q_weight,
    kv_weight,
    out_weight,
    head_gain,
    head_weight,
    head_bias,
    track_perm,
):
    n = lax.axis_size("tok")
    rows, width = hidden.shape[1], hidden.shape[2]
    head_dim = kv_weight.shape[1] // 2
    heads = q_weight.shape[1] // head_dim
    tracks = head_weight.shape[1]
    padded = -(-head_dim // LANES) * LANES
    line = n // 4
    kv_rows = kv_weight.shape[1] // LANES * rows
    bf16 = jnp.bfloat16
    vmem = pl.BlockSpec(memory_space=pltpu.VMEM)
    hbm = pl.BlockSpec(memory_space=pl.ANY)
    return pl.pallas_call(
        functools.partial(kernel, n),
        out_shape=jax.ShapeDtypeStruct((rows, tracks), jnp.float32),
        in_specs=[hbm, vmem, vmem, hbm, hbm, hbm, vmem, hbm, vmem, vmem],
        out_specs=vmem,
        scratch_shapes=[
            pltpu.VMEM(hidden.shape, bf16),
            pltpu.VMEM((2 * rows, width), bf16),
            pltpu.VMEM(kv_weight.shape, bf16),
            pltpu.VMEM(q_weight.shape, bf16),
            pltpu.VMEM((heads * padded, width), bf16),
            pltpu.VMEM(head_weight.shape, bf16),
            pltpu.VMEM((tracks, tracks), bf16),
            pltpu.VMEM((n, kv_rows + FLAG_ROWS, LANES), bf16),
            pltpu.VMEM((kv_rows + FLAG_ROWS, LANES), bf16),
            pltpu.VMEM((2 * rows, heads * padded), bf16),
            pltpu.VMEM((2 * rows, tracks), bf16),
            pltpu.VMEM((rows, tracks), bf16),
            pltpu.SemaphoreType.DMA((4,)),
            pltpu.SemaphoreType.DMA((heads,)),
            pltpu.SemaphoreType.DMA((2,)),
            pltpu.SemaphoreType.DMA((2,)),
            pltpu.SemaphoreType.DMA((1,)),
            pltpu.SemaphoreType.DMA((2,)),
            pltpu.SemaphoreType.DMA((n,)),
            pltpu.SemaphoreType.DMA((2, line)),
            pltpu.SemaphoreType.DMA((2, line)),
            pltpu.SemaphoreType.DMA((2, line)),
        ],
        compiler_params=pltpu.CompilerParams(
            collective_id=0, has_side_effects=True, vmem_limit_bytes=60 * 1024 * 1024
        ),
    )(
        hidden,
        base_ids,
        attn_gain,
        q_weight,
        kv_weight,
        out_weight,
        head_gain,
        head_weight,
        head_bias,
        track_perm,
    )


def solution(mesh):
    placed = (P("grp", "tok", None), P("grp", "tok"), P(), P(), P(), P(), P(), P(), P(), P())
    return jax.shard_map(
        per_device, mesh=mesh, in_specs=placed, out_specs=P(("grp", "tok"), None), check_vma=False
    )
```

```python
import functools
import math

import jax
import jax.numpy as jnp
from jax import lax
from jax.experimental import pallas as pl
from jax.experimental.pallas import tpu as pltpu
from jax.sharding import PartitionSpec as P

MESH = pl.DeviceIdType.MESH
LANES = 128
FLAG_ROWS = 16


def normalize(rows, gain):
    widened = rows.astype(jnp.float32)
    mean = jnp.mean(widened * widened, -1, keepdims=True)
    return (widened * lax.rsqrt(mean + 1e-06) * gain.astype(jnp.float32)).astype(jnp.bfloat16)


def dot(a, b):
    return jnp.dot(a, b, preferred_element_type=jnp.float32)


def dot_t(a, b):
    return lax.dot_general(a, b, (((1,), (1,)), ((), ())), preferred_element_type=jnp.float32)


def softplus(v):
    return jnp.maximum(v, 0.0) + jnp.log(1.0 + jnp.exp(-jnp.abs(v)))


def vector(ref):
    return ref[...].reshape(1, -1)


def kernel(
    n,
    hidden_ref,
    ids_ref,
    attn_gain_ref,
    q_hbm,
    kv_hbm,
    out_hbm,
    head_gain_ref,
    head_hbm,
    bias_ref,
    perm_ref,
    result_ref,
    hid,
    work,
    kv_w,
    q_w,
    out_w,
    head_w,
    perm_w,
    buf,
    stage,
    att,
    final,
    other,
    load_sem,
    out_sem,
    swap_send,
    work_sem,
    pair_sem,
    final_sem,
    recv,
    send_l,
    send_r,
    send_x,
):
    line = n // 4
    rows, width = hid.shape[1], hid.shape[2]
    both = 2 * rows
    tracks = head_w.shape[1]
    head_dim = kv_w.shape[1] // 2
    heads = q_w.shape[1] // head_dim
    padded = att.shape[1] // heads
    pad = padded - head_dim
    kv_tiles = kv_w.shape[1] // LANES
    me = lax.axis_index("tok")
    core = lax.rem(me, 2)
    x = lax.rem(me // 2, 2)
    z = me // 4
    left, right = me - 4, me + 4
    across, sibling = me + 2 - 4 * x, me + 1 - 2 * core
    mirror_zero, mirror_one = n - 2 - me + core, n - 1 - me + core
    first = core == 0
    second = core == 1
    has_left, has_right = z > 0, z < line - 1

    def slot(zc, xc, cc):
        return (xc * line + zc) * 2 + cc

    mine_at, pair_at = slot(z, x, core), slot(z, x, 1 - core)

    def remote(src, dst, send_sem, recv_sem, device):
        return pltpu.make_async_remote_copy(
            src_ref=src,
            dst_ref=dst,
            send_sem=send_sem,
            recv_sem=recv_sem,
            device_id={"tok": device},
            device_id_type=MESH,
        )

    load_hid = pltpu.make_async_copy(hidden_ref, hid, load_sem.at[0])
    load_kv = pltpu.make_async_copy(kv_hbm, kv_w, load_sem.at[1])
    load_q = pltpu.make_async_copy(q_hbm, q_w, load_sem.at[2])
    load_head = pltpu.make_async_copy(head_hbm, head_w, load_sem.at[3])
    load_out = [
        pltpu.make_async_copy(
            out_hbm.at[pl.ds(h * head_dim, head_dim)],
            out_w.at[pl.ds(h * padded + pad, head_dim)],
            out_sem.at[h],
        )
        for h in range(heads)
    ]
    for load in [load_hid, load_kv, load_q] + load_out + [load_head]:
        load.start()

    barrier = pltpu.get_barrier_semaphore()

    def greet(device):
        pl.semaphore_signal(barrier, inc=1, device_id={"tok": device}, device_id_type=MESH)

    greet(sibling)
    greet(across)
    pl.when(has_left)(lambda: greet(left))
    pl.when(has_right)(lambda: greet(right))

    @pl.when(second)
    def _():
        greet(mirror_zero)
        greet(mirror_one)

    peers = [flag.astype(jnp.int32) for flag in (has_left, has_right)]
    pl.semaphore_wait(barrier, 3 + sum(peers))

    cuts = work_sem.shape[1]
    cut = rows // cuts

    def share(strand, side, j, device):
        return remote(
            hidden_ref.at[strand, pl.ds(j * cut, cut)],
            work.at[pl.ds(side * rows + j * cut, cut)],
            swap_send.at[strand, j],
            work_sem.at[side, j],
            device,
        )

    def keep(j):
        return pltpu.make_async_copy(
            hidden_ref.at[0, pl.ds(j * cut, cut)],
            work.at[pl.ds(j * cut, cut)],
            work_sem.at[0, j],
        )

    def send_swap(j):
        pl.when(first)(lambda: share(1, 0, j, mirror_one).start())
        pl.when(second)(lambda: share(1, 1, j, mirror_one).start())

    @pl.when(first)
    def _():
        for j in range(cuts):
            keep(j).start()

    early = (cuts + 1) // 2
    for j in range(early):
        send_swap(j)

    def piece(index, device, send_sem):
        return remote(buf.at[index], buf.at[index], send_sem, recv.at[index], device)

    def to_left(zc, half):
        return piece(slot(zc, x, half), left, send_l.at[half, zc])

    def to_right(zc, half):
        return piece(slot(zc, x, half), right, send_r.at[half, zc])

    def to_across(zc, half):
        return piece(slot(zc, x, half), across, send_x.at[half, zc])

    pair = remote(stage, buf.at[mine_at], pair_sem.at[0], recv.at[mine_at], sibling)
    pair_in = remote(stage, buf.at[pair_at], pair_sem.at[0], recv.at[pair_at], sibling)

    out_zero = jnp.zeros((pad, width), jnp.bfloat16)
    for h in range(heads):
        out_w[pl.ds(h * padded, pad), :] = out_zero
    load_hid.wait()
    gain = vector(attn_gain_ref)
    normed = normalize(hid[...].reshape(both, width), gain)
    load_kv.wait()
    key_value = dot(normed, kv_w[...])
    forward, reverse = key_value[:rows], key_value[rows:]
    mine = jnp.where(first, forward, reverse).astype(jnp.bfloat16)
    theirs = jnp.where(first, reverse, forward).astype(jnp.bfloat16)
    flag = jnp.where(ids_ref[...] != 4, 1.0, 0.0).astype(jnp.float32)
    per_tile = LANES // rows
    lane = lax.broadcasted_iota(jnp.int32, (1, LANES), 1)
    start = lax.rem(mine_at, per_tile) * rows
    inside_tile = (lane >= start) & (lane < start + rows)

    def fill(block, values, flags):
        for j in range(kv_tiles):
            block[pl.ds(j * rows, rows), :] = values[:, j * LANES : (j + 1) * LANES]
        spread = jnp.where(inside_tile, jnp.concatenate([flags] * per_tile, axis=1), 0.0)
        spread = jnp.broadcast_to(spread, (FLAG_ROWS, LANES))
        block[pl.ds(kv_tiles * rows, FLAG_ROWS), :] = spread.astype(jnp.bfloat16)

    fill(stage, theirs, jnp.where(first, flag[1:2], flag[0:1]))
    pair.start()
    fill(buf.at[mine_at], mine, jnp.where(first, flag[0:1], flag[1:2]))

    def spread_out(zc, half, go_left, go_right):
        if go_left:
            pl.when(has_left)(lambda: to_left(zc, half).start())
        if go_right:
            pl.when(has_right)(lambda: to_right(zc, half).start())
        to_across(zc, half).start()

    spread_out(z, core, True, True)
    pair_in.wait_recv()
    spread_out(z, 1 - core, True, True)

    @pl.when(second)
    def _():
        for j in range(cuts):
            share(0, 1, j, sibling).start()

    late = cuts if line > 4 or line < 3 else min(early + 1, cuts)
    for j in range(early, late):
        send_swap(j)

    def hop(d):
        for k in range(2):
            half = core if k == 0 else 1 - core

            @pl.when(z - d >= 0)
            def _():
                to_right(z - d, half).wait_recv()
                spread_out(z - d, half, False, True)

            @pl.when(z + d < line)
            def _():
                to_left(z + d, half).wait_recv()
                spread_out(z + d, half, True, False)

    def project_queries(normed_rows):
        q = dot(normed_rows, q_w[...])
        pieces = []
        inside = lax.broadcasted_iota(jnp.int32, (both, padded), 1) < head_dim
        for h in range(heads):
            base = h * head_dim // LANES * LANES
            shift = h * head_dim - base
            window = q[:, base : base + padded]
            if shift:
                window = pltpu.roll(window, padded - shift, axis=1)
            pieces.append(jnp.where(inside, window, 0.0).astype(jnp.bfloat16))
        return pieces

    perm_row = vector(perm_ref)

    def build_perm(i, _):
        step = perm_w.shape[0] // 4
        chunk = 128
        for k in range(step // chunk):
            base = i * step + k * chunk
            ids = lax.broadcasted_iota(jnp.int32, (chunk, tracks), 0) + base
            hit = jnp.where(ids == perm_row, 1.0, 0.0)
            perm_w[pl.ds(pl.multiple_of(base, chunk), chunk), :] = hit.astype(jnp.bfloat16)
        return 0

    def make_queries():
        load_q.wait()
        for j in range(cuts):
            keep(j).wait()
            share(1, 1, j, mirror_one).wait_recv()
        return project_queries(normalize(work[...], gain))

    if line <= 4:
        for d in range(1, line):
            hop(d)
            if d == 1:
                for j in range(late, cuts):
                    send_swap(j)
                build_perm(0, 0)
                build_perm(1, 0)
            if d == line - 2:
                build_perm(2, 0)
                build_perm(3, 0)
    else:
        pl.loop(1, line)(hop)
    if not 3 <= line <= 4:
        lax.fori_loop(0, 4, build_perm, 0)
    queries = make_queries()

    blocks = 2 * line
    keys = blocks * rows
    scale = 1.0 / math.sqrt(head_dim)

    def part(column):
        at = pl.ds(column * blocks, blocks)

        def tiles(low, high):
            parts = [
                buf[at, pl.ds(j * rows, rows), :].reshape(keys, LANES) for j in range(low, high)
            ]
            return jnp.concatenate(parts, axis=1)

        flags = buf[at, pl.ds(kv_tiles * rows, FLAG_ROWS), :].astype(jnp.float32)
        parts = []
        for g in range(blocks // per_tile):
            row = flags[g * per_tile, 0:1, :]
            for k in range(1, per_tile):
                row = row + flags[g * per_tile + k, 0:1, :]
            parts.append(row)
        usable = jnp.concatenate(parts, axis=1) > 0.5
        lhs = tiles(0, padded // LANES)
        rhs = tiles(kv_tiles - padded // LANES, kv_tiles)
        states = []
        for h in range(heads):
            value = jnp.where(usable, dot_t(queries[h], lhs) * scale, -1e30)
            top = jnp.max(value, -1, keepdims=True)
            weight = jnp.where(usable, jnp.exp(value - top), 0.0)
            total = jnp.sum(weight, -1, keepdims=True)
            states.append((top, total, dot(weight.astype(jnp.bfloat16), rhs)))
        return states

    near = part(x)

    @pl.loop(0, line)
    def _(zc):
        for half in range(2):
            piece(slot(zc, 1 - x, half), across, send_x.at[half, zc]).wait_recv()

    distant = part(1 - x)
    inside = lax.broadcasted_iota(jnp.int32, (both, padded), 1) >= pad
    for h in range(heads):
        (top_a, total_a, sum_a), (top_b, total_b, sum_b) = near[h], distant[h]
        top = jnp.maximum(top_a, top_b)
        scale_a, scale_b = jnp.exp(top_a - top), jnp.exp(top_b - top)
        total = total_a * scale_a + total_b * scale_b
        mixed = (sum_a * scale_a + sum_b * scale_b) / total
        att[:, pl.ds(h * padded, padded)] = jnp.where(inside, mixed, 0.0).astype(jnp.bfloat16)

    for load in load_out:
        load.wait()
    residual = work[...].astype(jnp.float32) + dot(att[...], out_w[...])
    normed_out = normalize(residual, vector(head_gain_ref))
    load_head.wait()
    pred = softplus(dot(normed_out, head_w[...]) + vector(bias_ref)).astype(jnp.bfloat16)

    @pl.when(first)
    def _():
        final[...] = pred

    @pl.when(second)
    def _():
        flip = jnp.where(
            lax.broadcasted_iota(jnp.int32, (both, both), 0)
            + lax.broadcasted_iota(jnp.int32, (both, both), 1)
            == both - 1,
            1.0,
            0.0,
        ).astype(jnp.bfloat16)
        flipped = dot(flip, pred).astype(jnp.bfloat16)
        final[...] = flipped

    own = pl.ds(pl.multiple_of(core * rows, rows), rows)
    far = pl.ds(pl.multiple_of(rows - core * rows, rows), rows)
    exchange = remote(final.at[far], other, final_sem.at[0], final_sem.at[1], sibling)
    exchange.start()

    @pl.when(first)
    def _():
        exchange.wait_recv()
        result_ref[...] = 0.5 * (
            final[own, :].astype(jnp.float32) + dot(other[...], perm_w[...])
        )

    @pl.when(second)
    def _():
        turned = dot(final[own, :], perm_w[...])
        exchange.wait_recv()
        result_ref[...] = 0.5 * (other[...].astype(jnp.float32) + turned)

    exchange.wait_send()
    pair.wait_send()
    for j in range(cuts):
        share(1, 1, j, mirror_one).wait_send()
        pl.when(second)(lambda: share(0, 1, j, sibling).wait_send())

    @pl.loop(0, line)
    def _(zc):
        for half in range(2):
            pl.when(has_right & (zc <= z))(lambda: to_right(zc, half).wait_send())
            pl.when(has_left & (zc >= z))(lambda: to_left(zc, half).wait_send())
            to_across(zc, half).wait_send()


def per_device(
    hidden,
    base_ids,
    attn_gain,
    q_weight,
    kv_weight,
    out_weight,
    head_gain,
    head_weight,
    head_bias,
    track_perm,
):
    n = lax.axis_size("tok")
    rows, width = hidden.shape[1], hidden.shape[2]
    head_dim = kv_weight.shape[1] // 2
    heads = q_weight.shape[1] // head_dim
    tracks = head_weight.shape[1]
    padded = -(-head_dim // LANES) * LANES
    line = n // 4
    kv_rows = kv_weight.shape[1] // LANES * rows
    cuts = 4 if rows % 64 == 0 else 1
    bf16 = jnp.bfloat16
    vmem = pl.BlockSpec(memory_space=pltpu.VMEM)
    hbm = pl.BlockSpec(memory_space=pl.ANY)
    return pl.pallas_call(
        functools.partial(kernel, n),
        out_shape=jax.ShapeDtypeStruct((rows, tracks), jnp.float32),
        in_specs=[hbm, vmem, vmem, hbm, hbm, hbm, vmem, hbm, vmem, vmem],
        out_specs=vmem,
        scratch_shapes=[
            pltpu.VMEM(hidden.shape, bf16),
            pltpu.VMEM((2 * rows, width), bf16),
            pltpu.VMEM(kv_weight.shape, bf16),
            pltpu.VMEM(q_weight.shape, bf16),
            pltpu.VMEM((heads * padded, width), bf16),
            pltpu.VMEM(head_weight.shape, bf16),
            pltpu.VMEM((tracks, tracks), bf16),
            pltpu.VMEM((n, kv_rows + FLAG_ROWS, LANES), bf16),
            pltpu.VMEM((kv_rows + FLAG_ROWS, LANES), bf16),
            pltpu.VMEM((2 * rows, heads * padded), bf16),
            pltpu.VMEM((2 * rows, tracks), bf16),
            pltpu.VMEM((rows, tracks), bf16),
            pltpu.SemaphoreType.DMA((4,)),
            pltpu.SemaphoreType.DMA((heads,)),
            pltpu.SemaphoreType.DMA((2, cuts)),
            pltpu.SemaphoreType.DMA((2, cuts)),
            pltpu.SemaphoreType.DMA((1,)),
            pltpu.SemaphoreType.DMA((2,)),
            pltpu.SemaphoreType.DMA((n,)),
            pltpu.SemaphoreType.DMA((2, line)),
            pltpu.SemaphoreType.DMA((2, line)),
            pltpu.SemaphoreType.DMA((2, line)),
        ],
        compiler_params=pltpu.CompilerParams(
            collective_id=0, has_side_effects=True, vmem_limit_bytes=60 * 1024 * 1024
        ),
    )(
        hidden,
        base_ids,
        attn_gain,
        q_weight,
        kv_weight,
        out_weight,
        head_gain,
        head_weight,
        head_bias,
        track_perm,
    )


def solution(mesh):
    placed = (P("grp", "tok", None), P("grp", "tok"), P(), P(), P(), P(), P(), P(), P(), P())
    return jax.shard_map(
        per_device, mesh=mesh, in_specs=placed, out_specs=P(("grp", "tok"), None), check_vma=False
    )
```

```python
import functools
import math

import jax
import jax.numpy as jnp
from jax import lax
from jax.experimental import pallas as pl
from jax.experimental.pallas import tpu as pltpu
from jax.sharding import PartitionSpec as P

MESH = pl.DeviceIdType.MESH
LANES = 128
FLAG_ROWS = 16


def normalize(rows, gain):
    widened = rows.astype(jnp.float32)
    mean = jnp.mean(widened * widened, -1, keepdims=True)
    return (widened * lax.rsqrt(mean + 1e-06) * gain.astype(jnp.float32)).astype(jnp.bfloat16)


def dot(a, b):
    return jnp.dot(a, b, preferred_element_type=jnp.float32)


def dot_t(a, b):
    return lax.dot_general(a, b, (((1,), (1,)), ((), ())), preferred_element_type=jnp.float32)


def softplus(v):
    return jnp.maximum(v, 0.0) + jnp.log(1.0 + jnp.exp(-jnp.abs(v)))


def vector(ref):
    return ref[...].reshape(1, -1)


def kernel(
    n,
    hidden_ref,
    ids_ref,
    attn_gain_ref,
    q_hbm,
    kv_hbm,
    out_hbm,
    head_gain_ref,
    head_hbm,
    bias_ref,
    perm_ref,
    result_ref,
    hid,
    work,
    kv_w,
    q_w,
    out_w,
    head_w,
    perm_w,
    buf,
    stage,
    att,
    final,
    other,
    load_sem,
    out_sem,
    swap_send,
    work_sem,
    pair_sem,
    final_sem,
    recv,
    send_l,
    send_r,
    send_x,
):
    line = n // 4
    rows, width = hid.shape[1], hid.shape[2]
    both = 2 * rows
    tracks = head_w.shape[1]
    head_dim = kv_w.shape[1] // 2
    heads = q_w.shape[1] // head_dim
    padded = att.shape[1] // heads
    pad = padded - head_dim
    kv_tiles = kv_w.shape[1] // LANES
    me = lax.axis_index("tok")
    core = lax.rem(me, 2)
    x = lax.rem(me // 2, 2)
    z = me // 4
    left, right = me - 4, me + 4
    across, sibling = me + 2 - 4 * x, me + 1 - 2 * core
    mirror_zero, mirror_one = n - 2 - me + core, n - 1 - me + core
    first = core == 0
    second = core == 1
    has_left, has_right = z > 0, z < line - 1

    def slot(zc, xc, cc):
        return (xc * line + zc) * 2 + cc

    mine_at, pair_at = slot(z, x, core), slot(z, x, 1 - core)

    def remote(src, dst, send_sem, recv_sem, device):
        return pltpu.make_async_remote_copy(
            src_ref=src,
            dst_ref=dst,
            send_sem=send_sem,
            recv_sem=recv_sem,
            device_id={"tok": device},
            device_id_type=MESH,
        )

    load_hid = pltpu.make_async_copy(hidden_ref, hid, load_sem.at[0])
    load_kv = pltpu.make_async_copy(kv_hbm, kv_w, load_sem.at[1])
    load_q = pltpu.make_async_copy(q_hbm, q_w, load_sem.at[2])
    load_head = pltpu.make_async_copy(head_hbm, head_w, load_sem.at[3])
    load_out = [
        pltpu.make_async_copy(
            out_hbm.at[pl.ds(h * head_dim, head_dim)],
            out_w.at[pl.ds(h * padded + pad, head_dim)],
            out_sem.at[h],
        )
        for h in range(heads)
    ]
    for load in [load_hid, load_kv, load_q] + load_out + [load_head]:
        load.start()

    barrier = pltpu.get_barrier_semaphore()

    def greet(device):
        pl.semaphore_signal(barrier, inc=1, device_id={"tok": device}, device_id_type=MESH)

    greet(sibling)
    greet(across)
    pl.when(has_left)(lambda: greet(left))
    pl.when(has_right)(lambda: greet(right))

    @pl.when(second)
    def _():
        greet(mirror_zero)
        greet(mirror_one)

    peers = [flag.astype(jnp.int32) for flag in (has_left, has_right)]
    pl.semaphore_wait(barrier, 3 + sum(peers))

    cuts = work_sem.shape[1]
    cut = rows // cuts

    def share(strand, side, j, device):
        return remote(
            hidden_ref.at[strand, pl.ds(j * cut, cut)],
            work.at[pl.ds(side * rows + j * cut, cut)],
            swap_send.at[strand, j],
            work_sem.at[side, j],
            device,
        )

    def keep(j):
        return pltpu.make_async_copy(
            hidden_ref.at[0, pl.ds(j * cut, cut)],
            work.at[pl.ds(j * cut, cut)],
            work_sem.at[0, j],
        )

    def send_swap(j):
        pl.when(first)(lambda: share(1, 0, j, mirror_one).start())
        pl.when(second)(lambda: share(1, 1, j, mirror_one).start())

    @pl.when(first)
    def _():
        for j in range(cuts):
            keep(j).start()

    early = 1
    for j in range(early):
        send_swap(j)

    def piece(index, device, send_sem):
        return remote(buf.at[index], buf.at[index], send_sem, recv.at[index], device)

    def to_left(zc, half):
        return piece(slot(zc, x, half), left, send_l.at[half, zc])

    def to_right(zc, half):
        return piece(slot(zc, x, half), right, send_r.at[half, zc])

    def to_across(zc, half):
        return piece(slot(zc, x, half), across, send_x.at[half, zc])

    pair = remote(stage, buf.at[mine_at], pair_sem.at[0], recv.at[mine_at], sibling)
    pair_in = remote(stage, buf.at[pair_at], pair_sem.at[0], recv.at[pair_at], sibling)

    out_zero = jnp.zeros((pad, width), jnp.bfloat16)
    for h in range(heads):
        out_w[pl.ds(h * padded, pad), :] = out_zero
    load_hid.wait()
    gain = vector(attn_gain_ref)
    normed = normalize(hid[...].reshape(both, width), gain)
    load_kv.wait()
    key_value = dot(normed, kv_w[...])
    forward, reverse = key_value[:rows], key_value[rows:]
    mine = jnp.where(first, forward, reverse).astype(jnp.bfloat16)
    theirs = jnp.where(first, reverse, forward).astype(jnp.bfloat16)
    flag = jnp.where(ids_ref[...] != 4, 1.0, 0.0).astype(jnp.float32)
    per_tile = LANES // rows
    lane = lax.broadcasted_iota(jnp.int32, (1, LANES), 1)
    start = lax.rem(mine_at, per_tile) * rows
    inside_tile = (lane >= start) & (lane < start + rows)

    def fill(block, values, flags):
        for j in range(kv_tiles):
            block[pl.ds(j * rows, rows), :] = values[:, j * LANES : (j + 1) * LANES]
        spread = jnp.where(inside_tile, jnp.concatenate([flags] * per_tile, axis=1), 0.0)
        spread = jnp.broadcast_to(spread, (FLAG_ROWS, LANES))
        block[pl.ds(kv_tiles * rows, FLAG_ROWS), :] = spread.astype(jnp.bfloat16)

    fill(stage, theirs, jnp.where(first, flag[1:2], flag[0:1]))
    pair.start()
    fill(buf.at[mine_at], mine, jnp.where(first, flag[0:1], flag[1:2]))

    def spread_out(zc, half, go_left, go_right):
        if go_left:
            pl.when(has_left)(lambda: to_left(zc, half).start())
        if go_right:
            pl.when(has_right)(lambda: to_right(zc, half).start())
        to_across(zc, half).start()

    spread_out(z, core, True, True)
    pair_in.wait_recv()
    spread_out(z, 1 - core, True, True)

    @pl.when(second)
    def _():
        for j in range(cuts):
            share(0, 1, j, sibling).start()

    late = cuts if line > 4 or line < 3 else min(early + 2, cuts)
    for j in range(early, late):
        send_swap(j)

    def hop(d):
        for k in range(2):
            half = core if k == 0 else 1 - core

            @pl.when(z - d >= 0)
            def _():
                to_right(z - d, half).wait_recv()
                spread_out(z - d, half, False, True)

            @pl.when(z + d < line)
            def _():
                to_left(z + d, half).wait_recv()
                spread_out(z + d, half, True, False)

    def project_queries(normed_rows):
        q = dot(normed_rows, q_w[...])
        pieces = []
        inside = lax.broadcasted_iota(jnp.int32, (both, padded), 1) < head_dim
        for h in range(heads):
            base = h * head_dim // LANES * LANES
            shift = h * head_dim - base
            window = q[:, base : base + padded]
            if shift:
                window = pltpu.roll(window, padded - shift, axis=1)
            pieces.append(jnp.where(inside, window, 0.0).astype(jnp.bfloat16))
        return pieces

    perm_row = vector(perm_ref)

    def build_perm(i, _):
        step = perm_w.shape[0] // 4
        chunk = 128
        for k in range(step // chunk):
            base = i * step + k * chunk
            ids = lax.broadcasted_iota(jnp.int32, (chunk, tracks), 0) + base
            hit = jnp.where(ids == perm_row, 1.0, 0.0)
            perm_w[pl.ds(pl.multiple_of(base, chunk), chunk), :] = hit.astype(jnp.bfloat16)
        return 0

    def make_queries():
        load_q.wait()
        for j in range(cuts):
            keep(j).wait()
            share(1, 1, j, mirror_one).wait_recv()
        return project_queries(normalize(work[...], gain))

    if line <= 4:
        for d in range(1, line):
            hop(d)
            if d == 1:
                for j in range(late, cuts):
                    send_swap(j)
                build_perm(0, 0)
                build_perm(1, 0)
            if d == line - 2:
                build_perm(2, 0)
                build_perm(3, 0)
    else:
        pl.loop(1, line)(hop)
    if not 3 <= line <= 4:
        lax.fori_loop(0, 4, build_perm, 0)
    queries = make_queries()

    blocks = 2 * line
    keys = blocks * rows
    scale = 1.0 / math.sqrt(head_dim)

    def part(column):
        at = pl.ds(column * blocks, blocks)

        def tiles(low, high):
            parts = [
                buf[at, pl.ds(j * rows, rows), :].reshape(keys, LANES) for j in range(low, high)
            ]
            return jnp.concatenate(parts, axis=1)

        flags = buf[at, pl.ds(kv_tiles * rows, FLAG_ROWS), :].astype(jnp.float32)
        parts = []
        for g in range(blocks // per_tile):
            row = flags[g * per_tile, 0:1, :]
            for k in range(1, per_tile):
                row = row + flags[g * per_tile + k, 0:1, :]
            parts.append(row)
        usable = jnp.concatenate(parts, axis=1) > 0.5
        lhs = tiles(0, padded // LANES)
        rhs = tiles(kv_tiles - padded // LANES, kv_tiles)
        states = []
        for h in range(heads):
            value = jnp.where(usable, dot_t(queries[h], lhs) * scale, -1e30)
            top = jnp.max(value, -1, keepdims=True)
            weight = jnp.where(usable, jnp.exp(value - top), 0.0)
            total = jnp.sum(weight, -1, keepdims=True)
            states.append((top, total, dot(weight.astype(jnp.bfloat16), rhs)))
        return states

    near = part(x)

    @pl.loop(0, line)
    def _(zc):
        for half in range(2):
            piece(slot(zc, 1 - x, half), across, send_x.at[half, zc]).wait_recv()

    distant = part(1 - x)
    inside = lax.broadcasted_iota(jnp.int32, (both, padded), 1) >= pad
    for h in range(heads):
        (top_a, total_a, sum_a), (top_b, total_b, sum_b) = near[h], distant[h]
        top = jnp.maximum(top_a, top_b)
        scale_a, scale_b = jnp.exp(top_a - top), jnp.exp(top_b - top)
        total = total_a * scale_a + total_b * scale_b
        mixed = (sum_a * scale_a + sum_b * scale_b) / total
        att[:, pl.ds(h * padded, padded)] = jnp.where(inside, mixed, 0.0).astype(jnp.bfloat16)

    for load in load_out:
        load.wait()
    residual = work[...].astype(jnp.float32) + dot(att[...], out_w[...])
    normed_out = normalize(residual, vector(head_gain_ref))
    load_head.wait()
    pred = softplus(dot(normed_out, head_w[...]) + vector(bias_ref)).astype(jnp.bfloat16)

    @pl.when(first)
    def _():
        final[...] = pred

    @pl.when(second)
    def _():
        flip = jnp.where(
            lax.broadcasted_iota(jnp.int32, (both, both), 0)
            + lax.broadcasted_iota(jnp.int32, (both, both), 1)
            == both - 1,
            1.0,
            0.0,
        ).astype(jnp.bfloat16)
        flipped = dot(flip, pred).astype(jnp.bfloat16)
        final[...] = flipped

    own = pl.ds(pl.multiple_of(core * rows, rows), rows)
    far = pl.ds(pl.multiple_of(rows - core * rows, rows), rows)
    exchange = remote(final.at[far], other, final_sem.at[0], final_sem.at[1], sibling)
    exchange.start()

    @pl.when(first)
    def _():
        exchange.wait_recv()
        result_ref[...] = 0.5 * (
            final[own, :].astype(jnp.float32) + dot(other[...], perm_w[...])
        )

    @pl.when(second)
    def _():
        turned = dot(final[own, :], perm_w[...])
        exchange.wait_recv()
        result_ref[...] = 0.5 * (other[...].astype(jnp.float32) + turned)

    exchange.wait_send()
    pair.wait_send()
    for j in range(cuts):
        share(1, 1, j, mirror_one).wait_send()
        pl.when(second)(lambda: share(0, 1, j, sibling).wait_send())

    @pl.loop(0, line)
    def _(zc):
        for half in range(2):
            pl.when(has_right & (zc <= z))(lambda: to_right(zc, half).wait_send())
            pl.when(has_left & (zc >= z))(lambda: to_left(zc, half).wait_send())
            to_across(zc, half).wait_send()


def per_device(
    hidden,
    base_ids,
    attn_gain,
    q_weight,
    kv_weight,
    out_weight,
    head_gain,
    head_weight,
    head_bias,
    track_perm,
):
    n = lax.axis_size("tok")
    rows, width = hidden.shape[1], hidden.shape[2]
    head_dim = kv_weight.shape[1] // 2
    heads = q_weight.shape[1] // head_dim
    tracks = head_weight.shape[1]
    padded = -(-head_dim // LANES) * LANES
    line = n // 4
    kv_rows = kv_weight.shape[1] // LANES * rows
    cuts = 4 if rows % 64 == 0 else 1
    bf16 = jnp.bfloat16
    vmem = pl.BlockSpec(memory_space=pltpu.VMEM)
    hbm = pl.BlockSpec(memory_space=pl.ANY)
    return pl.pallas_call(
        functools.partial(kernel, n),
        out_shape=jax.ShapeDtypeStruct((rows, tracks), jnp.float32),
        in_specs=[hbm, vmem, vmem, hbm, hbm, hbm, vmem, hbm, vmem, vmem],
        out_specs=vmem,
        scratch_shapes=[
            pltpu.VMEM(hidden.shape, bf16),
            pltpu.VMEM((2 * rows, width), bf16),
            pltpu.VMEM(kv_weight.shape, bf16),
            pltpu.VMEM(q_weight.shape, bf16),
            pltpu.VMEM((heads * padded, width), bf16),
            pltpu.VMEM(head_weight.shape, bf16),
            pltpu.VMEM((tracks, tracks), bf16),
            pltpu.VMEM((n, kv_rows + FLAG_ROWS, LANES), bf16),
            pltpu.VMEM((kv_rows + FLAG_ROWS, LANES), bf16),
            pltpu.VMEM((2 * rows, heads * padded), bf16),
            pltpu.VMEM((2 * rows, tracks), bf16),
            pltpu.VMEM((rows, tracks), bf16),
            pltpu.SemaphoreType.DMA((4,)),
            pltpu.SemaphoreType.DMA((heads,)),
            pltpu.SemaphoreType.DMA((2, cuts)),
            pltpu.SemaphoreType.DMA((2, cuts)),
            pltpu.SemaphoreType.DMA((1,)),
            pltpu.SemaphoreType.DMA((2,)),
            pltpu.SemaphoreType.DMA((n,)),
            pltpu.SemaphoreType.DMA((2, line)),
            pltpu.SemaphoreType.DMA((2, line)),
            pltpu.SemaphoreType.DMA((2, line)),
        ],
        compiler_params=pltpu.CompilerParams(
            collective_id=0, has_side_effects=True, vmem_limit_bytes=60 * 1024 * 1024
        ),
    )(
        hidden,
        base_ids,
        attn_gain,
        q_weight,
        kv_weight,
        out_weight,
        head_gain,
        head_weight,
        head_bias,
        track_perm,
    )


def solution(mesh):
    placed = (P("grp", "tok", None), P("grp", "tok"), P(), P(), P(), P(), P(), P(), P(), P())
    return jax.shard_map(
        per_device, mesh=mesh, in_specs=placed, out_specs=P(("grp", "tok"), None), check_vma=False
    )
```
